256 devices in a mesh: dp: 4 (over z_hi, core), seq: 64 (over x, z_lo, y).
Axes of the slice: x: 4, y: 4, z: 8 (z_hi: 2, z_lo: 4; z = z_hi * 4 + z_lo), core: 2. Of those that a mesh axis runs over, the one named last changes fastest.
Arguments:
- query_space: bfloat16 [4, 64, 256, 1152], P('dp', 'seq'), may hold values from -8 to 8
- key_space: bfloat16 [4, 64, 256, 1152], P('dp', 'seq'), may hold values from -8 to 8
- value_space: bfloat16 [4, 64, 256, 1152], P('dp', 'seq'), may hold values from -6 to 6
- query_time: bfloat16 [4, 64, 256, 1152], P('dp', None, 'seq'), may hold values from -8 to 8
- key_time: bfloat16 [4, 64, 256, 1152], P('dp', None, 'seq'), may hold values from -8 to 8
- value_time: bfloat16 [4, 64, 256, 1152], P('dp', None, 'seq'), may hold values from -6 to 6
- cotangent: bfloat16 [4, 64, 256, 1152], P('dp', 'seq'), may hold values from -16 to 16
- gate_space: float32 [4, 1152], P('dp'), may hold values from 0.3 to 3
- gate_time: float32 [4, 1152], P('dp'), may hold values from 0.3 to 3
- weight_space: bfloat16 [1152, 1152], replicated, may hold values from -0.1875 to 0.1875
- weight_time: bfloat16 [1152, 1152], replicated, may hold values from -0.1875 to 0.1875
Outputs:
- gradient_query_space: bfloat16 [4, 64, 256, 1152], P('dp', 'seq')
- gradient_key_space: bfloat16 [4, 64, 256, 1152], P('dp', 'seq')
- gradient_value_space: bfloat16 [4, 64, 256, 1152], P('dp', 'seq')
- gradient_query_time: bfloat16 [4, 64, 256, 1152], P('dp', 'seq')
- gradient_key_time: bfloat16 [4, 64, 256, 1152], P('dp', 'seq')
- gradient_value_time: bfloat16 [4, 64, 256, 1152], P('dp', 'seq')
- gradient_weight_space: float32 [1152, 1152], P('seq', 'dp')
- gradient_weight_time: float32 [1152, 1152], P('seq', 'dp')
The draws below stay inside these ranges and needn't reach their ends.
All inputs are finite; a program needn't handle non-finite values.
Results may differ from the reference program's by a relative error of at most 0.013.
Values may be sent and summed in bfloat16 or wider, within the bound.
A program may use at most 128 MiB of HBM per device.

```python
import math
import jax
import jax.numpy as jnp
from jax import lax

HEADS = 16
HEAD_DIM = 72
D = 1152
CELLS = 256
FRAMES = 64
SAMPLES = 4


def draw_query_space(key, part):
    key = jax.random.fold_in(key, 1)
    shape = (SAMPLES, FRAMES, CELLS, D)
    return jax.random.truncated_normal(key, -6.0, 6.0, shape, jnp.float32).astype(jnp.bfloat16)


def draw_key_space(key, part):
    key = jax.random.fold_in(key, 2)
    shape = (SAMPLES, FRAMES, CELLS, D)
    return jax.random.truncated_normal(key, -6.0, 6.0, shape, jnp.float32).astype(jnp.bfloat16)


def draw_query_time(key, part):
    key = jax.random.fold_in(key, 3)
    shape = (SAMPLES, FRAMES, CELLS, D)
    return jax.random.truncated_normal(key, -6.0, 6.0, shape, jnp.float32).astype(jnp.bfloat16)


def draw_key_time(key, part):
    key = jax.random.fold_in(key, 4)
    shape = (SAMPLES, FRAMES, CELLS, D)
    return jax.random.truncated_normal(key, -6.0, 6.0, shape, jnp.float32).astype(jnp.bfloat16)


def spiked(values, own_key, source, target, parts, factor):
    owner, partner = [(jnp.arange(values.shape[dim]) // (values.shape[dim] // parts)).reshape([-1 if axis == dim else 1 for axis in range(values.ndim)]) for dim in (source, target)]
    chosen = jax.random.permutation(own_key, parts)[partner]
    strong = (owner == chosen) | (owner == (partner + parts // 2) % parts)
    return jnp.where(strong, factor * values, values)


def shard_levels(key, shape, shards, smallest, largest):
    loudness, own = 1.0, jax.random.fold_in(key, 6)
    for axis_at, blocks in shards:
        heights = jnp.exp(jax.random.uniform(jax.random.fold_in(own, axis_at), (blocks,), jnp.float32, smallest / len(shards), largest / len(shards)))
        loudness = loudness * jnp.repeat(heights, shape[axis_at] // blocks).reshape([-1 if axis == axis_at else 1 for axis in range(len(shape))])
    return loudness


def noise(own_key, dims, scale, reach, split=(), dtype=jnp.bfloat16):
    entries = jax.random.normal(own_key, dims, jnp.float32) * scale
    if len(split) > 0:
        entries = shard_levels(own_key, dims, split, -0.22, 0.18) * entries
    return jnp.clip(entries, min=-reach, max=reach).astype(dtype)


def noise_with(rng, dims, deviation, limit, pieces, heavy, held_as=jnp.bfloat16):
    drawn = deviation * jax.random.normal(rng, dims, jnp.float32)
    if pieces:
        drawn = drawn * shard_levels(rng, dims, pieces, -0.22, 0.18)
    return jnp.clip(spiked(drawn, jax.random.fold_in(rng, 3), *heavy), -limit, limit).astype(held_as)


def setup_inputs(seed: int = 0) -> dict:
    key_list = jax.random.split(jax.random.key(seed), 12)
    return {
        "query_space": draw_query_space(jax.random.fold_in(key_list[11], 71), 0),
        "key_space": draw_key_space(jax.random.fold_in(key_list[11], 71), 0),
        "value_space": noise(key_list[2], (SAMPLES, FRAMES, CELLS, D), 1.0, 6.0, ((0, 4), (1, 64))),
        "query_time": draw_query_time(jax.random.fold_in(key_list[11], 71), 0),
        "key_time": draw_key_time(jax.random.fold_in(key_list[11], 71), 0),
        "value_time": noise(key_list[5], (SAMPLES, FRAMES, CELLS, D), 1.0, 6.0, ((0, 4), (2, 64))),
        "cotangent": noise_with(key_list[6], (SAMPLES, FRAMES, CELLS, D), 1.0, 16.0, ((0, 4), (1, 64)), (1, 3, 64, 4.0)),
        "gate_space": jnp.clip(jnp.exp(math.log(3.0) - 2.3025851 * jax.random.uniform(key_list[7], (SAMPLES, D), jnp.float32) ** shard_levels(key_list[7], (SAMPLES, D), ((0, 4),), -0.2, 0.2)), 0.3, 3.0),
        "gate_time": jnp.clip(jnp.exp(math.log(3.0) - 2.3025851 * jax.random.uniform(key_list[8], (SAMPLES, D), jnp.float32) ** shard_levels(key_list[8], (SAMPLES, D), ((0, 4),), -0.2, 0.2)), 0.3, 3.0),
        "weight_space": noise(key_list[9], (D, D), D ** -0.5, 0.1875),
        "weight_time": noise(key_list[10], (D, D), D ** -0.5, 0.1875),
    }


def attention_backward(queries, keyset, values, upstream):
    wide = jnp.float32
    factor = 1.0 / math.sqrt(queries.shape[-1])
    scores = jnp.einsum('blche,bmche->bchlm', queries.astype(wide), keyset.astype(wide)) * factor
    highest = lax.optimization_barrier(jnp.max(scores, axis=-1, keepdims=True))
    raised = jnp.exp(scores - highest)
    shares = raised / lax.optimization_barrier(jnp.sum(raised, axis=-1, keepdims=True))
    shares_half = shares.astype(jnp.bfloat16)
    attended = jnp.einsum('bchlm,bmche->blche', shares_half.astype(wide), values.astype(wide)).astype(jnp.bfloat16)
    share_grad = jnp.einsum('blche,bmche->bchlm', upstream.astype(wide), values.astype(wide))
    centre = lax.optimization_barrier(jnp.sum(shares * share_grad, axis=-1, keepdims=True))
    score_grad = (shares * (share_grad - centre) * factor).astype(jnp.bfloat16)
    query_grad = jnp.einsum('bchlm,bmche->blche', score_grad.astype(wide), keyset.astype(wide)).astype(jnp.bfloat16)
    key_grad = jnp.einsum('bchlm,blche->bmche', score_grad.astype(wide), queries.astype(wide)).astype(jnp.bfloat16)
    value_grad = jnp.einsum('bchlm,blche->bmche', shares_half.astype(wide), upstream.astype(wide)).astype(jnp.bfloat16)
    return (query_grad, key_grad, value_grad, attended)

def project(gated, weight):
    rows = gated.reshape(-1, gated.shape[-1])
    result = jnp.dot(rows, weight.T, preferred_element_type=jnp.float32)
    return result.astype(jnp.bfloat16).reshape(gated.shape)

def reference(query_space, key_space, value_space, query_time, key_time, value_time, cotangent, gate_space, gate_time, weight_space, weight_time):
    wide = jnp.float32
    gated_space = (gate_space[:, None, None, :].astype(wide) * cotangent.astype(wide)).astype(jnp.bfloat16)
    gated_time = (gate_time[:, None, None, :].astype(wide) * cotangent.astype(wide)).astype(jnp.bfloat16)
    upstream_space = project(gated_space, weight_space)
    upstream_time = project(gated_time, weight_time)
    full_shape = cotangent.shape

    def frame_view(array):
        return array.reshape(SAMPLES * FRAMES, 1, CELLS, 1, HEADS, HEAD_DIM)

    def one_frame(items):
        return attention_backward(items[0], items[1], items[2], items[3])
    spatial = lax.map(one_frame, (frame_view(query_space), frame_view(key_space), frame_view(value_space), frame_view(upstream_space)))
    spatial = tuple((item.reshape(full_shape) for item in spatial))

    def video_view(array):
        return array.reshape(SAMPLES, 1, FRAMES, CELLS, HEADS, HEAD_DIM)
    temporal = lax.map(one_frame, (video_view(query_time), video_view(key_time), video_view(value_time), video_view(upstream_time)))
    temporal = tuple((item.reshape(full_shape) for item in temporal))
    rows = SAMPLES * FRAMES * CELLS
    factor = 1.0 / math.sqrt(rows)
    weight_grad_space = jnp.dot(spatial[3].reshape(rows, D).T, gated_space.reshape(rows, D), preferred_element_type=jnp.float32) * factor
    weight_grad_time = jnp.dot(temporal[3].reshape(rows, D).T, gated_time.reshape(rows, D), preferred_element_type=jnp.float32) * factor
    return (spatial[0], spatial[1], spatial[2], temporal[0], temporal[1], temporal[2], weight_grad_space, weight_grad_time)
```

```python
import functools
import math

import jax
import jax.numpy as jnp
import numpy as np
from jax import lax
from jax.experimental import pallas as pl
from jax.experimental.pallas import tpu as pltpu
from jax.sharding import PartitionSpec as P

HEADS = 16
HEAD_DIM = 72
D = HEADS * HEAD_DIM
CELL = 4
WIN = 256
MESH = pl.DeviceIdType.MESH
F32 = jnp.float32
BF16 = jnp.bfloat16
CHUNK_HEADS = 5


def padded(rows):
    return -(-rows // 16) * 16


def row_maps(n):
    xz, y, c = np.meshgrid(np.arange(n * n), np.arange(n), np.arange(CELL), indexing="ij")
    index = {
        "N": ((xz * n + y) * CELL + c).reshape(-1),
        "C": ((c * n * n + xz) * n + y).reshape(-1),
        "P": ((y * n * n + xz) * CELL + c).reshape(-1),
    }
    tokens = n * n * n * CELL

    def perm(source, target):
        out = np.zeros((tokens, tokens), np.float32)
        out[index[target], index[source]] = 1.0
        return out

    rows_x = D // n
    rows_y = rows_x // n
    rows_z = rows_y // n
    pad_y, pad_z = padded(rows_y), padded(rows_z)
    first = np.zeros((n * pad_y, n * rows_x), np.float32)
    second = np.zeros((n * pad_z, n * pad_y), np.float32)
    third = np.zeros((pad_z, n * pad_z), np.float32)
    for source in range(n):
        for yy in range(n):
            for zz in range(n):
                for r in range(rows_z):
                    first[yy * pad_y + zz * rows_z + r, source * rows_x + (zz * n + yy) * rows_z + r] = 1.0
        for zz in range(n):
            for r in range(rows_z):
                second[zz * pad_z + r, source * pad_y + zz * rows_z + r] = 1.0
        for r in range(rows_z):
            third[r, source * pad_z + r] = 1.0
    made = [perm("N", "P"), perm("P", "C"), perm("N", "C"), perm("C", "P"), perm("P", "N"), first, second, third]
    return [m.astype(jnp.bfloat16) for m in made]


def dot(a, b):
    return lax.dot_general(a, b, (((1,), (0,)), ((), ())), preferred_element_type=F32)


def dot_rows(a, b):
    return lax.dot_general(a, b, (((0,), (0,)), ((), ())), preferred_element_type=F32)


def dot_lanes(a, b):
    return lax.dot_general(a, b, (((1,), (1,)), ((), ())), preferred_element_type=F32)


def head_mask(head, start, width):
    lane = lax.broadcasted_iota(jnp.int32, (1, width), 1) + start
    inside = (lane >= head * HEAD_DIM) & (lane < (head + 1) * HEAD_DIM)
    return jnp.where(inside, 1.0, 0.0).astype(BF16)


def lane_chunks(width, step):
    return [(start, min(step, width - start)) for start in range(0, width, step)]


def permute(matrix, source, target):
    for start, size in lane_chunks(D, 384):
        target[:, start : start + size] = dot(matrix[...], source[:, start : start + size]).astype(BF16)


def project(gated, weight, target):
    def step(i, _):
        at = pl.ds(pl.multiple_of(i * 384, 128), 384)
        target[:, at] = dot_lanes(gated[...], weight[at, :]).astype(BF16)
        return 0

    lax.fori_loop(0, D // 384, step, 0)


def softmax_and_grad(scores, grads):
    factor = math.log2(math.e) / math.sqrt(HEAD_DIM)
    highest = jnp.max(scores, axis=0, keepdims=True)
    raised = jnp.exp2((scores - highest) * factor)
    shares = raised * (1.0 / jnp.sum(raised, axis=0, keepdims=True))
    centre = jnp.sum(shares * grads, axis=0, keepdims=True)
    return shares.astype(BF16), (shares * (grads - centre)).astype(BF16)


def window(head):
    start = jnp.minimum(head * HEAD_DIM // 128, (D - WIN) // 128) * 128
    return pl.multiple_of(start, 128)


def scores_space(q, k, v, u, shares, grads):
    def step(head, _):
        start = window(head)
        at = pl.ds(start, WIN)
        mask = head_mask(head, start, WIN)
        scores = dot_lanes(k[:, at] * mask, q[:, at])
        share_grad = dot_lanes(v[:, at] * mask, u[:, at])
        shares[head], grads[head] = softmax_and_grad(scores, share_grad)
        return 0

    lax.fori_loop(0, HEADS, step, 0)


def scores_time(q, k, v, u, shares, grads):
    tokens = q.shape[0]
    half, frames = tokens // 2, tokens // CELL
    lane = lax.broadcasted_iota(jnp.int32, (1, half), 1)
    low = lane < frames
    cell_of_lane = lax.broadcasted_iota(jnp.int32, (1, tokens), 1) // frames

    def compact(a, b):
        parts = []
        for i in range(2):
            rows = slice(i * half, (i + 1) * half)
            block = dot_lanes(a[rows, :], b[rows, :])
            parts.append(jnp.where(low, block[:frames, :], block[frames:, :]))
        return jnp.concatenate(parts, axis=1)

    def expand(block):
        zero = jnp.zeros_like(block)
        return jnp.concatenate([jnp.where(cell_of_lane == c, block, zero) for c in range(CELL)], axis=0)

    def step(head, _):
        start = window(head)
        at = pl.ds(start, WIN)
        mask = head_mask(head, start, WIN)
        scores = compact(k[:, at] * mask, q[:, at])
        share_grad = compact(v[:, at] * mask, u[:, at])
        share, grad = softmax_and_grad(scores, share_grad)
        shares[head] = expand(share)
        grads[head] = expand(grad)
        return 0

    lax.fori_loop(0, HEADS, step, 0)


def gradients(q, k, v, u, shares, grads, attended, dq, dk, dv):
    factor = 1.0 / math.sqrt(HEAD_DIM)

    def chunk(first, heads, start, width):
        at = pl.ds(start, width)
        totals = [None] * 4
        for i in range(heads):
            head = first + i
            mask = head_mask(head, start, width)
            terms = (
                dot_rows(shares[head], v[:, at] * mask),
                dot_rows(grads[head], k[:, at] * mask),
                dot(grads[head], q[:, at] * mask),
                dot(shares[head], u[:, at] * mask),
            )
            totals = [term if total is None else total + term for total, term in zip(totals, terms)]
        attended[:, at] = totals[0].astype(BF16)
        dq[:, at] = (totals[1] * factor).astype(BF16)
        dk[:, at] = (totals[2] * factor).astype(BF16)
        dv[:, at] = totals[3].astype(BF16)

    def step(i, _):
        start = pl.multiple_of(i * WIN, 128)
        chunk(start // HEAD_DIM, CHUNK_HEADS, start, WIN)
        return 0

    whole = D // WIN
    lax.fori_loop(0, whole, step, 0)
    tail = whole * WIN
    chunk(tail // HEAD_DIM, HEADS - tail // HEAD_DIM, tail, D - tail)


def kernel(
    n,
    tokens_total,
    qs_h,
    ks_h,
    vs_h,
    qt_h,
    kt_h,
    vt_h,
    cot_h,
    ws_h,
    wt_h,
    np_h,
    pc_h,
    nc_h,
    cp_h,
    pn_h,
    first_h,
    second_h,
    third_h,
    gate_s,
    gate_t,
    dqs_o,
    dks_o,
    dvs_o,
    dqt_o,
    dkt_o,
    dvt_o,
    gws_o,
    gwt_o,
    qs,
    ks,
    vs,
    qraw,
    kraw,
    vraw,
    cot,
    ws,
    wt,
    m_np,
    m_pc,
    m_nc,
    m_cp,
    m_pn,
    m_first,
    m_second,
    m_third,
    wide,
    qt,
    kt,
    vt,
    rc1,
    mid,
    rc2,
    cot_c,
    gated,
    attended,
    up,
    shares,
    grads,
    spatial,
    temporal,
    sent,
    got_y,
    turned,
    far_a,
    far_g,
    product,
    got_x,
    send_y,
    got_wy,
    send_z,
    got_wz,
    send_h,
    got_h,
    send_c,
    got_c,
    load_sem,
    store_sem,
    own_sem,
    c1_send,
    c1_recv,
    c2_send,
    c2_recv,
    ty_send,
    ty_recv,
    tx_send,
    tx_recv,
    w_send,
    w_recv,
    pair_send,
    pair_recv,
):
    dp = lax.axis_index("dp")
    seq = lax.axis_index("seq")
    groups = n * n
    group, y = seq // n, seq % n
    x, z = group // n, group % n
    core = dp % 2
    sibling = dp + 1 - 2 * core
    partner = (dp + 2) % 4
    rows_g = n * CELL
    rows_y = groups * CELL

    loads = [
        pltpu.make_async_copy(source, target, load_sem.at[i])
        for i, (source, target) in enumerate(
            (
                (cot_h, cot),
                (ws_h, ws),
                (qs_h, qs),
                (ks_h, ks),
                (vs_h, vs),
                (qt_h, qraw),
                (kt_h, kraw),
                (vt_h, vraw),
                (wt_h, wt),
                (np_h, m_np),
                (pc_h, m_pc),
                (nc_h, m_nc),
                (cp_h, m_cp),
                (pn_h, m_pn),
                (first_h, m_first),
                (second_h, m_second),
                (third_h, m_third),
            )
        )
    ]
    for load in loads:
        load.start()

    def group_peer(g):
        return (dp, g * n + y)

    def y_peer(yy):
        return (dp, group * n + yy)

    def x_peer(xx):
        return (dp, (xx * n + z) * n + y)

    def z_peer(zz):
        return (dp, (x * n + zz) * n + y)

    barrier = pltpu.get_barrier_semaphore()

    def greet(device):
        pl.semaphore_signal(barrier, inc=1, device_id=device, device_id_type=MESH)

    def greet_group(i, _):
        greet(group_peer((group + i) % groups))
        return 0

    lax.fori_loop(1, groups, greet_group, 0)
    for i in range(1, n):
        greet(y_peer((y + i) % n))
    greet((sibling, seq))
    greet((partner, seq))
    pl.semaphore_wait(barrier, groups - 1 + n - 1 + 2)

    def exchange(size, me, device, source, target, send, recv):
        def copy(i):
            peer = (me + i) % size
            return pltpu.make_async_remote_copy(
                src_ref=source(peer),
                dst_ref=target(me),
                send_sem=send(i),
                recv_sem=recv(i),
                device_id=device(peer),
                device_id_type=MESH,
            )

        def start():
            def step(i, _):
                copy(i).start()
                return 0

            lax.fori_loop(1, size, step, 0)

        def wait_recv():
            def step(i, _):
                copy(i).wait_recv()
                return 0

            lax.fori_loop(1, size, step, 0)

        def wait_send():
            def step(i, _):
                copy(i).wait_send()
                return 0

            lax.fori_loop(1, size, step, 0)

        return start, wait_recv, wait_send

    def rows(ref, at, count):
        return ref.at[pl.ds(pl.multiple_of(at * count, 16 if count % 16 == 0 else 8), count)]

    sends = []

    loads[0].wait()
    c1_start, c1_wait, c1_done = exchange(
        groups,
        group,
        group_peer,
        lambda g: rows(cot, g, rows_g),
        lambda g: rows(rc1, g, rows_g),
        lambda i: c1_send.at[i],
        lambda i: c1_recv.at[i],
    )
    c1_start()
    sends.append(c1_done)
    own1 = pltpu.make_async_copy(rows(cot, group, rows_g), rows(rc1, group, rows_g), own_sem.at[0])
    own1.start()

    gated[0] = (gate_s[...] * cot[...].astype(F32)).astype(BF16)
    loads[1].wait()
    project(gated.at[0], ws, up)
    for load in loads[2:5]:
        load.wait()
    scores_space(qs, ks, vs, up, shares, grads)

    loads[11].wait()
    for raw, target, load in ((qraw, qt, loads[5]), (kraw, kt, loads[6]), (vraw, vt, loads[7])):
        load.wait()

        def widen(i, _):
            pair = jnp.concatenate([raw[2 * i].astype(F32), raw[2 * i + 1].astype(F32)], axis=0)
            wide[pl.ds(pl.multiple_of(i * 8, 8), 8), :] = pair
            return 0

        lax.fori_loop(0, raw.shape[0] // 2, widen, 0)
        for start, size in lane_chunks(D, 384):
            part = wide[:, start : start + size].astype(BF16)
            target[:, start : start + size] = dot(m_nc[...], part).astype(BF16)

    own1.wait()
    c1_wait()
    loads[9].wait()
    permute(m_np, rc1, mid)
    c2_start, c2_wait, c2_done = exchange(
        n,
        y,
        y_peer,
        lambda yy: rows(mid, yy, rows_y),
        lambda yy: rows(rc2, yy, rows_y),
        lambda i: c2_send.at[i],
        lambda i: c2_recv.at[i],
    )
    c2_start()
    sends.append(c2_done)
    own2 = pltpu.make_async_copy(rows(mid, y, rows_y), rows(rc2, y, rows_y), own_sem.at[1])
    own2.start()

    gradients(qs, ks, vs, up, shares, grads, attended.at[0], spatial.at[0], spatial.at[1], spatial.at[2])
    stores = [
        pltpu.make_async_copy(spatial.at[i], out, store_sem.at[i]) for i, out in enumerate((dqs_o, dks_o, dvs_o))
    ]
    for store in stores:
        store.start()

    own2.wait()
    c2_wait()
    loads[10].wait()
    permute(m_pc, rc2, cot_c)
    gated[1] = (gate_t[...] * cot_c[...].astype(F32)).astype(BF16)
    loads[8].wait()
    project(gated.at[1], wt, up)
    scores_time(qt, kt, vt, up, shares, grads)
    gradients(qt, kt, vt, up, shares, grads, attended.at[1], temporal.at[0], temporal.at[1], temporal.at[2])

    loads[12].wait()
    outs = (dqt_o, dkt_o, dvt_o)
    first_steps = []
    for i in range(3):
        permute(m_cp, temporal.at[i], sent.at[i])
        start, wait, done = exchange(
            n,
            y,
            y_peer,
            lambda yy, i=i: rows(sent.at[i], yy, rows_y),
            lambda yy, i=i: rows(got_y.at[i], yy, rows_y),
            lambda k, i=i: ty_send.at[i * n + k],
            lambda k, i=i: ty_recv.at[i * n + k],
        )
        start()
        sends.append(done)
        own = pltpu.make_async_copy(rows(sent.at[i], y, rows_y), rows(got_y.at[i], y, rows_y), own_sem.at[2 + i])
        own.start()
        first_steps.append((own, wait))

    pair = [
        pltpu.make_async_remote_copy(
            src_ref=source.at[1 - core],
            dst_ref=target,
            send_sem=pair_send.at[i],
            recv_sem=pair_recv.at[i],
            device_id=(sibling, seq),
            device_id_type=MESH,
        )
        for i, (source, target) in enumerate(((attended, far_a), (gated, far_g)))
    ]
    for copy in pair:
        copy.start()

    loads[13].wait()
    last_steps = []
    for i in range(3):
        own, wait = first_steps[i]
        own.wait()
        wait()
        permute(m_pn, got_y.at[i], turned.at[i])
        start, wait, done = exchange(
            groups,
            group,
            group_peer,
            lambda g, i=i: rows(turned.at[i], g, rows_g),
            lambda g, i=i: rows(outs[i], g, rows_g),
            lambda k, i=i: tx_send.at[i * groups + k],
            lambda k, i=i: tx_recv.at[i * groups + k],
        )
        start()
        sends.append(done)
        own = pltpu.make_async_copy(rows(turned.at[i], group, rows_g), rows(outs[i], group, rows_g), own_sem.at[5 + i])
        own.start()
        last_steps.append((own, wait))

    for copy in pair:
        copy.wait_recv()
    scale = 1.0 / math.sqrt(tokens_total)

    def multiply(i, _):
        at = pl.ds(pl.multiple_of(i * 128, 128), 128)
        near, far = attended[core, :, at], far_a[:, at]
        for start, size in lane_chunks(D, 384):
            to = slice(start, start + size)
            total = dot_rows(near, gated[core, :, to]) + dot_rows(far, far_g[:, to])
            product[at, to] = (total * scale).astype(BF16)
        return 0

    lax.fori_loop(0, D // 128, multiply, 0)

    def reduce(size, me, device, source, target, slot, matrix, result, own):
        count = target.shape[0] // size
        start, wait, done = exchange(
            size,
            me,
            device,
            lambda peer: rows(source, peer, count),
            lambda peer: rows(target, peer, count),
            lambda k: w_send.at[slot * n + k],
            lambda k: w_recv.at[slot * n + k],
        )
        start()
        sends.append(done)
        near = pltpu.make_async_copy(rows(source, me, count), rows(target, me, count), own)
        near.start()
        near.wait()
        wait()
        for at, width in lane_chunks(D, 384):
            result[:, at : at + width] = dot(matrix[...], target[:, at : at + width]).astype(BF16)

    for load in loads[14:]:
        load.wait()
    reduce(n, x, x_peer, product, got_x, 0, m_first, send_y, own_sem.at[8])
    reduce(n, y, y_peer, send_y, got_wy, 1, m_second, send_z, own_sem.at[9])
    reduce(n, z, z_peer, send_z, got_wz, 2, m_third, send_h, own_sem.at[10])

    def swap(source, target, slot, device):
        copy = pltpu.make_async_remote_copy(
            src_ref=source,
            dst_ref=target,
            send_sem=pair_send.at[slot],
            recv_sem=pair_recv.at[slot],
            device_id=device,
            device_id_type=MESH,
        )
        copy.start()
        copy.wait_recv()
        return copy

    pair.append(swap(send_h, got_h, 2, (partner, seq)))
    send_c[...] = (send_h[...].astype(F32) + got_h[...].astype(F32)).astype(BF16)
    pair.append(swap(send_c, got_c, 3, (sibling, seq)))
    count, width = gws_o.shape
    for i in range(4):

        @pl.when(dp == i)
        def _():
            at = slice(i * width, (i + 1) * width)
            near = send_c[...].astype(F32)[:count, at]
            far = got_c[...].astype(F32)[:count, at]
            gws_o[...] = far if i % 2 else near
            gwt_o[...] = near if i % 2 else far

    for own, wait in last_steps:
        own.wait()
        wait()
    for store in stores:
        store.wait()
    for done in sends:
        done()
    for copy in pair:
        copy.wait_send()


def per_device(n, maps, qs, ks, vs, qt, kt, vt, cot, gate_s, gate_t, ws, wt):
    tokens = cot.shape[2]
    frames = qt.shape[1]
    groups = n * n
    pad_y, pad_z = padded(D // n // n), padded(D // n // n // n)
    shape = cot.shape
    flat = lambda a: a.reshape(tokens, D)
    cells = lambda a: a.reshape(frames, CELL, D)
    any_space = pl.BlockSpec(memory_space=pl.ANY)
    vmem = pl.BlockSpec(memory_space=pltpu.VMEM)
    token = pltpu.VMEM((tokens, D), BF16)
    tokens_of = lambda k: pltpu.VMEM((k, tokens, D), BF16)
    square = pltpu.VMEM((tokens, tokens), BF16)
    raw = pltpu.VMEM((frames, CELL, D), BF16)
    weight = pltpu.VMEM((D, D), BF16)
    dma = lambda k: pltpu.SemaphoreType.DMA((k,))
    small = pltpu.VMEM((pad_z, D), BF16)
    total = 4 * n**3 * tokens
    out_rows, out_columns = D // n**3, D // 4
    result = pl.pallas_call(
        functools.partial(kernel, n, total),
        out_shape=[jax.ShapeDtypeStruct((tokens, D), BF16)] * 6
        + [jax.ShapeDtypeStruct((out_rows, out_columns), F32)] * 2,
        in_specs=[any_space] * 17 + [vmem] * 2,
        out_specs=[any_space] * 6 + [vmem] * 2,
        scratch_shapes=[token] * 3
        + [raw] * 3
        + [token]
        + [weight] * 2
        + [square] * 5
        + [pltpu.VMEM(m.shape, BF16) for m in maps[5:]]
        + [pltpu.VMEM((tokens, D), F32)]
        + [token] * 3
        + [token] * 4
        + [tokens_of(2)] * 2
        + [token]
        + [pltpu.VMEM((HEADS, tokens, tokens), BF16)] * 2
        + [tokens_of(3)] * 5
        + [token] * 2
        + [weight] * 2
        + [pltpu.VMEM((n * pad_y, D), BF16)] * 2
        + [pltpu.VMEM((n * pad_z, D), BF16)] * 2
        + [small] * 4
        + [dma(17), dma(3), dma(11)]
        + [dma(groups)] * 2
        + [dma(n)] * 2
        + [dma(3 * n)] * 2
        + [dma(3 * groups)] * 2
        + [dma(3 * n)] * 2
        + [dma(4)] * 2,
        compiler_params=pltpu.CompilerParams(
            collective_id=0, has_side_effects=True, vmem_limit_bytes=60 * 1024 * 1024
        ),
    )(flat(qs), flat(ks), flat(vs), cells(qt), cells(kt), cells(vt), flat(cot), ws, wt, *maps, gate_s, gate_t)
    return tuple(a.reshape(shape) for a in result[:6]) + tuple(result[6:])


def solution(mesh):
    n = round(mesh.shape["seq"] ** (1 / 3))
    maps = row_maps(n)
    frames = P("dp", "seq", None, None)
    cells = P("dp", None, "seq", None)

    def run(*args):
        return per_device(n, [jnp.asarray(m) for m in maps], *args)

    return jax.shard_map(
        run,
        mesh=mesh,
        in_specs=(frames,) * 3 + (cells,) * 3 + (frames, P("dp", None), P("dp", None), P(), P()),
        out_specs=(frames,) * 6 + (P("seq", "dp"),) * 2,
        check_vma=False,
    )
```

```python
import functools
import math

import jax
import jax.numpy as jnp
import numpy as np
from jax import lax
from jax.experimental import pallas as pl
from jax.experimental.pallas import tpu as pltpu
from jax.sharding import PartitionSpec as P

HEADS = 16
HEAD_DIM = 72
D = HEADS * HEAD_DIM
CELL = 4
WIN = 256
MESH = pl.DeviceIdType.MESH
F32 = jnp.float32
BF16 = jnp.bfloat16
CHUNK_HEADS = 5


def padded(rows):
    return -(-rows // 16) * 16


def row_maps(n):
    rows_x = D // n
    rows_y = rows_x // n
    rows_z = rows_y // n
    pad_y, pad_z = padded(rows_y), padded(rows_z)
    turn = np.zeros((D, D), np.float32)
    first_x = np.zeros((n * pad_y, D), np.float32)
    first_y = np.zeros((n * pad_y, D), np.float32)
    second = np.zeros((n * pad_z, n * pad_y), np.float32)
    r = np.arange(rows_z)
    for i in range(n):
        for zz in range(n):
            for j in range(n):
                turn[((j * n + i) * n + zz) * rows_z + r, ((i * n + zz) * n + j) * rows_z + r] = 1.0
                first_x[j * pad_y + zz * rows_z + r, i * rows_x + (zz * n + j) * rows_z + r] = 1.0
                first_y[j * pad_y + zz * rows_z + r, i * rows_x + (j * n + zz) * rows_z + r] = 1.0
            second[zz * pad_z + r, i * pad_y + zz * rows_z + r] = 1.0
    return [m.astype(jnp.bfloat16) for m in (turn, first_x, first_y, second)]


def dot(a, b):
    return lax.dot_general(a, b, (((1,), (0,)), ((), ())), preferred_element_type=F32)


def dot_rows(a, b):
    return lax.dot_general(a, b, (((0,), (0,)), ((), ())), preferred_element_type=F32)


def dot_lanes(a, b):
    return lax.dot_general(a, b, (((1,), (1,)), ((), ())), preferred_element_type=F32)


def head_mask(head, start, width):
    lane = lax.broadcasted_iota(jnp.int32, (1, width), 1) + start
    inside = (lane >= head * HEAD_DIM) & (lane < (head + 1) * HEAD_DIM)
    return jnp.where(inside, 1.0, 0.0).astype(BF16)


def lane_chunks(width, step):
    return [(start, min(step, width - start)) for start in range(0, width, step)]


def project(gated, weight, target, start, width):
    at = pl.ds(start, width)
    target[:, at] = dot_lanes(gated[...], weight[at, :]).astype(BF16)


def softmax_and_grad(scores, grads):
    factor = math.log2(math.e) / math.sqrt(HEAD_DIM)
    highest = jnp.max(scores, axis=0, keepdims=True)
    raised = jnp.exp2((scores - highest) * factor)
    shares = raised * (1.0 / jnp.sum(raised, axis=0, keepdims=True))
    centre = jnp.sum(shares * grads, axis=0, keepdims=True)
    return shares.astype(BF16), (shares * (grads - centre)).astype(BF16)


def window(head):
    start = jnp.minimum(head * HEAD_DIM // 128, (D - WIN) // 128) * 128
    return pl.multiple_of(start, 128)


def scores_space(q, k, v, u, shares, grads):
    def step(head, _):
        start = window(head)
        at = pl.ds(start, WIN)
        mask = head_mask(head, start, WIN)
        scores = dot_lanes(k[:, at] * mask, q[:, at])
        share_grad = dot_lanes(v[:, at] * mask, u[:, at])
        shares[head], grads[head] = softmax_and_grad(scores, share_grad)
        return 0

    lax.fori_loop(0, HEADS, step, 0, unroll=4)


def score_time(head, q, k, v, u, shares, grads):
    tokens = q.shape[0]
    half, frames = tokens // 2, tokens // CELL
    low = lax.broadcasted_iota(jnp.int32, (1, half), 1) < frames
    cell_of_lane = lax.broadcasted_iota(jnp.int32, (1, tokens), 1) // frames
    start = window(head)
    at = pl.ds(start, WIN)
    mask = head_mask(head, start, WIN)

    def compact(a, b):
        parts = []
        for i in range(2):
            rows = slice(i * half, (i + 1) * half)
            block = dot_lanes(a[rows, :], b[rows, :])
            parts.append(jnp.where(low, block[:frames, :], block[frames:, :]))
        return jnp.concatenate(parts, axis=1)

    def expand(block):
        zero = jnp.zeros_like(block)
        return jnp.concatenate([jnp.where(cell_of_lane == c, block, zero) for c in range(CELL)], axis=0)

    scores = compact(k[:, at] * mask, q[:, at])
    share_grad = compact(v[:, at] * mask, u[:, at])
    share, grad = softmax_and_grad(scores, share_grad)
    shares[head] = expand(share)
    grads[head] = expand(grad)


def gradients(first, heads, start, width, q, k, v, u, shares, grads):
    factor = 1.0 / math.sqrt(HEAD_DIM)
    at = pl.ds(start, width)
    totals = [None] * 4
    for i in range(heads):
        head = first + i
        mask = head_mask(head, start, width)
        terms = (
            dot_rows(shares[head], v[:, at] * mask),
            dot_rows(grads[head], k[:, at] * mask),
            dot(grads[head], q[:, at] * mask),
            dot(shares[head], u[:, at] * mask),
        )
        totals = [term if total is None else total + term for total, term in zip(totals, terms)]
    return totals[0], totals[1] * factor, totals[2] * factor, totals[3]


def to_slabs(source, target, count):
    def step(i, _):
        wide = source[pl.ds(pl.multiple_of(i * 16, 16), 16), :].astype(F32)
        for j in range(16 // CELL):
            target[i * (16 // CELL) + j] = wide[j * CELL : (j + 1) * CELL, :].astype(BF16)
        return 0

    lax.fori_loop(0, count * CELL // 16, step, 0, unroll=2)


def slabs_to_cells(source, wide):
    frames = source.shape[0]

    def step(f, _):
        slab = source[f].astype(F32)
        for t in range(D // 128):
            wide[t, pl.ds(f, CELL, stride=frames), :] = slab[:, t * 128 : (t + 1) * 128]
        return 0

    lax.fori_loop(0, frames, step, 0, unroll=8)


def kernel(
    n,
    tokens_total,
    qs_h,
    ks_h,
    vs_h,
    qt_h,
    kt_h,
    vt_h,
    cot_h,
    ws_h,
    wt_h,
    turn_h,
    first_x_h,
    first_y_h,
    second_h,
    gate_s,
    gate_t,
    dqs_o,
    dks_o,
    dvs_o,
    dqt_o,
    dkt_o,
    dvt_o,
    gws_o,
    gwt_o,
    qs,
    ks,
    vs,
    qraw,
    kraw,
    vraw,
    cot,
    ws,
    wt,
    turn,
    first_x,
    first_y,
    second,
    wide,
    parts,
    qt,
    kt,
    vt,
    cot_slabs,
    cot_got,
    gated,
    attended,
    up,
    shares,
    grads,
    spatial,
    temporal,
    sent,
    got,
    far_a,
    far_g,
    product,
    turned,
    got_1x,
    got_1y,
    send_2x,
    send_2y,
    got_2x,
    got_2y,
    send_z,
    got_z,
    send_h,
    got_h,
    send_c,
    got_c,
    load_sem,
    store_sem,
    own_sem,
    cot_send,
    cot_recv,
    t_send,
    t_recv,
    w_send,
    w_recv,
    pair_send,
    pair_recv,
):
    dp = lax.axis_index("dp")
    seq = lax.axis_index("seq")
    devices = n * n * n
    group, y = seq // n, seq % n
    x, z = group // n, group % n
    core, side = dp % 2, dp // 2
    sibling = dp + 1 - 2 * core
    partner = (dp + 2) % 4
    tokens = devices * CELL
    split = product.shape[1] - got_1y.shape[1]

    loads = [
        pltpu.make_async_copy(source, target, load_sem.at[i])
        for i, (source, target) in enumerate(
            (
                (cot_h, cot),
                (ws_h, ws),
                (qs_h, qs),
                (ks_h, ks),
                (vs_h, vs),
                (qt_h, qraw),
                (kt_h, kraw),
                (vt_h, vraw),
                (wt_h, wt),
                (turn_h, turn),
                (first_x_h, first_x),
                (first_y_h, first_y),
                (second_h, second),
            )
        )
    ]
    for load in loads:
        load.start()

    def seq_peer(s):
        return (dp, s)

    def y_peer(yy):
        return (dp, group * n + yy)

    def x_peer(xx):
        return (dp, (xx * n + z) * n + y)

    def z_peer(zz):
        return (dp, (x * n + zz) * n + y)

    barrier = pltpu.get_barrier_semaphore()

    def greet(device):
        pl.semaphore_signal(barrier, inc=1, device_id=device, device_id_type=MESH)

    def greet_seq(i, _):
        greet(seq_peer((seq + i) % devices))
        return 0

    lax.fori_loop(1, devices, greet_seq, 0)
    greet((sibling, seq))
    greet((partner, seq))
    loads[0].wait()
    to_slabs(cot, cot_slabs, devices)
    pl.semaphore_wait(barrier, devices - 1 + 2)

    def remote(source, target, send, recv, device):
        return pltpu.make_async_remote_copy(
            src_ref=source,
            dst_ref=target,
            send_sem=send,
            recv_sem=recv,
            device_id=device,
            device_id_type=MESH,
        )

    def local(source, target, sem):
        return pltpu.make_async_copy(source, target, sem)

    def send_cot(i, _):
        peer = (seq + i) % devices
        remote(cot_slabs.at[peer], cot_got.at[seq], cot_send.at[0], cot_recv.at[0], seq_peer(peer)).start()
        return 0

    lax.fori_loop(1, devices, send_cot, 0)
    cot_own = local(cot_slabs.at[seq], cot_got.at[seq], own_sem.at[0])
    cot_own.start()

    gated[0] = (gate_s[...] * cot[...].astype(F32)).astype(BF16)
    loads[1].wait()
    for start, width in lane_chunks(D, 384):
        project(gated.at[0], ws, up, start, width)
    for load in loads[2:5]:
        load.wait()
    scores_space(qs, ks, vs, up, shares, grads)
    whole = D // WIN
    tail = whole * WIN

    def space_window(first, heads, start, width):
        at = pl.ds(start, width)
        total = gradients(first, heads, start, width, qs, ks, vs, up, shares, grads)
        attended[0, :, at] = total[0].astype(BF16)
        for i in range(3):
            spatial[i, :, at] = total[1 + i].astype(BF16)

    def space_step(i, _):
        start = pl.multiple_of(i * WIN, 128)
        space_window(start // HEAD_DIM, CHUNK_HEADS, start, WIN)
        return 0

    lax.fori_loop(0, whole, space_step, 0)
    space_window(tail // HEAD_DIM, HEADS - tail // HEAD_DIM, tail, D - tail)

    def pair_copies(kind):
        return [
            remote(source.at[kind], target, pair_send.at[i], pair_recv.at[i], (sibling, seq))
            for i, (source, target) in enumerate(((attended, far_a), (gated, far_g)))
        ]

    @pl.when(core == 1)
    def _():
        for copy in pair_copies(0):
            copy.start()

    stores = [local(spatial.at[i], out, store_sem.at[i]) for i, out in enumerate((dqs_o, dks_o, dvs_o))]
    for store in stores:
        store.start()

    for raw, target, load in ((qraw, qt, loads[5]), (kraw, kt, loads[6]), (vraw, vt, loads[7])):
        load.wait()
        slabs_to_cells(raw, wide)
        for t in range(D // 128):
            target[:, t * 128 : (t + 1) * 128] = wide[t].astype(BF16)

    def rows(ref, at, count):
        return ref.at[pl.ds(pl.multiple_of(at * count, 16 if count % 16 == 0 else 8), count)]

    def exchange(me, device, source, target, slot):
        copies = []
        for i in range(1, n):
            peer = (me + i) % n
            k = slot * n + i
            copies.append(remote(source(peer), target(me), w_send.at[k], w_recv.at[k], device(peer)))
        own = local(source(me), target(me), own_sem.at[1 + slot])
        return own, copies

    count_1, count_2 = D // n, send_2x.shape[0] // n
    lanes_1 = slice(0, split)
    steps = (
        exchange(x, x_peer, lambda p: rows(product, p, count_1).at[:, lanes_1], lambda p: rows(got_1x, p, count_1), 0),
        exchange(y, y_peer, lambda p: rows(turned, p, count_1), lambda p: rows(got_1y, p, count_1), 1),
        exchange(y, y_peer, lambda p: rows(send_2x, p, count_2), lambda p: rows(got_2x, p, count_2), 2),
        exchange(x, x_peer, lambda p: rows(send_2y, p, count_2), lambda p: rows(got_2y, p, count_2), 3),
        exchange(z, z_peer, lambda p: send_z.at[p], lambda p: got_z.at[p], 4),
    )

    def begin(step):
        own, copies = step
        for copy in copies:
            copy.start()
        own.start()

    def arrived(step):
        own, copies = step
        own.wait()
        for copy in copies:
            copy.wait_recv()

    scale = 1.0 / math.sqrt(tokens_total)

    def weight_product():
        for copy in pair_copies(0):
            copy.wait_recv()

        def multiply(start, width):
            to = slice(start, start + width)

            def step(i, _):
                at = pl.ds(pl.multiple_of(i * 128, 128), 128)
                total = dot_rows(attended[core, :, at], gated[core, :, to]) + dot_rows(far_a[:, at], far_g[:, to])
                product[at, to] = (total * scale).astype(BF16)
                return 0

            lax.fori_loop(0, D // 128, step, 0, unroll=3)

        multiply(0, split)
        begin(steps[0])
        multiply(split, D - split)
        loads[9].wait()

        def turn_rows(i, _):
            at = pl.ds(pl.multiple_of(i * 128, 128), 128)
            turned[at, :] = dot(turn[at, :], product[:, split:]).astype(BF16)
            return 0

        lax.fori_loop(0, D // 128, turn_rows, 0, unroll=3)
        begin(steps[1])

    def weight_second():
        for at, load, matrix, source, target in (
            (0, loads[10], first_x, got_1x, send_2x),
            (1, loads[11], first_y, got_1y, send_2y),
        ):
            load.wait()
            arrived(steps[at])
            for start, width in lane_chunks(target.shape[1], 384):
                lanes = slice(start, start + width)
                target[:, lanes] = dot(matrix[...], source[:, lanes]).astype(BF16)
            begin(steps[2 + at])

    def weight_third():
        loads[12].wait()
        pad, count = second.shape[0] // n, send_z.shape[1]
        for at, source, base in ((2, got_2x, 0), (3, got_2y, split)):
            arrived(steps[at])
            for start, width in lane_chunks(source.shape[1], 384):
                total = dot(second[...], source[:, start : start + width]).astype(BF16)
                for i in range(n):
                    send_z[i, :, base + start : base + start + width] = total[i * pad : i * pad + count, :]
        begin(steps[4])

    half = got_h.shape[1]
    step_h = D - half

    def half_of(ref, which):
        return ref.at[:, pl.ds(pl.multiple_of(which * step_h, 128), half)]

    side_copy = remote(half_of(send_h, 1 - side), got_h, pair_send.at[2], pair_recv.at[2], (partner, seq))
    core_copy = remote(send_c, got_c, pair_send.at[3], pair_recv.at[3], (sibling, seq))

    def weight_fourth():
        arrived(steps[4])
        total = got_z[0].astype(F32)
        for i in range(1, n):
            total = total + got_z[i].astype(F32)
        send_h[...] = total.astype(BF16)
        side_copy.start()

    def weight_fifth():
        side_copy.wait_recv()
        near = send_h[:, pl.ds(pl.multiple_of(side * step_h, 128), half)].astype(F32)
        send_c[...] = (near + got_h[...].astype(F32)).astype(BF16)
        core_copy.start()

    def weight_last():
        core_copy.wait_recv()
        width = gws_o.shape[1]
        for i in range(4):

            @pl.when(dp == i)
            def _():
                base = i * width - (i // 2) * step_h
                near = send_c[...].astype(F32)[:, base : base + width]
                far = got_c[...].astype(F32)[:, base : base + width]
                gws_o[...] = far if i % 2 else near
                gwt_o[...] = near if i % 2 else far

    @pl.when(core == 0)
    def _():
        weight_product()

    cot_own.wait()
    rest = pl.ds(0, devices - 1)
    local(cot_got.at[rest], cot_got.at[rest], cot_recv.at[0]).wait()
    slabs_to_cells(cot_got, wide)
    for t in range(D // 128):
        at = slice(t * 128, (t + 1) * 128)
        gated[1, :, at] = (gate_t[:, at] * wide[t]).astype(BF16)
    loads[8].wait()

    def time_window(i, first, heads, start, width):
        at = pl.ds(start, width)
        total = gradients(first, heads, start, width, qt, kt, vt, up, shares, grads)
        attended[1, :, at] = total[0].astype(BF16)
        tiles = width // 128
        for t in range(3):
            for j in range(tiles):
                parts[t * tiles + j] = total[1 + t][:, j * 128 : (j + 1) * 128]

        def narrow(f, _):
            for t in range(3):
                for j in range(tiles):
                    to = pl.ds(pl.multiple_of(start + j * 128, 128), 128)
                    sent[f, t, :, to] = parts[t * tiles + j, pl.ds(f, CELL, stride=devices), :].astype(BF16)
            return 0

        lax.fori_loop(0, devices, narrow, 0, unroll=8)

        def send(k, _):
            peer = (seq + k) % devices
            remote(
                sent.at[peer, :, :, at], got.at[seq, :, :, at], t_send.at[i], t_recv.at[i], seq_peer(peer)
            ).start()
            return 0

        lax.fori_loop(1, devices, send, 0)
        local(sent.at[seq, :, :, at], got.at[seq, :, :, at], own_sem.at[6 + i]).start()

    def time_step(i, _):
        @pl.when(i < D // 384)
        def _():
            project(gated.at[1], wt, up, pl.multiple_of(i * 384, 128), 384)

        for j in range(HEADS // whole):
            score_time(i * (HEADS // whole) + j, qt, kt, vt, up, shares, grads)
        start = pl.multiple_of(i * WIN, 128)
        time_window(i, start // HEAD_DIM, CHUNK_HEADS, start, WIN)
        return 0

    lax.fori_loop(0, whole, time_step, 0)
    time_window(whole, tail // HEAD_DIM, HEADS - tail // HEAD_DIM, tail, D - tail)

    @pl.when(core == 0)
    def _():
        for copy in pair_copies(1):
            copy.start()
        weight_second()

    @pl.when(core == 1)
    def _():
        weight_product()
        weight_second()

    weight_third()
    weight_fourth()
    weight_fifth()

    windows = lane_chunks(D, WIN)
    for i, (start, width) in enumerate(windows):
        at = slice(start, start + width)
        local(sent.at[seq, :, :, at], got.at[seq, :, :, at], own_sem.at[6 + i]).wait()
        piece = got.at[rest, :, :, at]
        local(piece, piece, t_recv.at[i]).wait()

        def join(k, _):
            for t in range(3):
                slabs = [got[k * (16 // CELL) + j, t, :, at].astype(F32) for j in range(16 // CELL)]
                to = pl.ds(pl.multiple_of(k * 16, 16), 16)
                temporal[t, to, at] = jnp.concatenate(slabs, axis=0).astype(BF16)
            return 0

        lax.fori_loop(0, tokens // 16, join, 0, unroll=2)
    final = [local(temporal.at[i], out, store_sem.at[3 + i]) for i, out in enumerate((dqt_o, dkt_o, dvt_o))]
    for store in final:
        store.start()

    weight_last()
    for store in stores + final:
        store.wait()
    local(cot_slabs.at[rest], cot_slabs.at[rest], cot_send.at[0]).wait()
    for i, (start, width) in enumerate(windows):
        piece = sent.at[rest, :, :, start : start + width]
        local(piece, piece, t_send.at[i]).wait()
    for _, copies in steps:
        for copy in copies:
            copy.wait_send()
    for copy in pair_copies(0) + [side_copy, core_copy]:
        copy.wait_send()


def per_device(n, maps, qs, ks, vs, qt, kt, vt, cot, gate_s, gate_t, ws, wt):
    tokens = cot.shape[2]
    frames = qt.shape[1]
    devices = n * n * n
    rows_z = D // devices
    pad_y = padded(D // n // n)
    split = 640
    half = D // 2 + 64
    shape = cot.shape
    flat = lambda a: a.reshape(tokens, D)
    cells = lambda a: a.reshape(frames, CELL, D)
    any_space = pl.BlockSpec(memory_space=pl.ANY)
    vmem = pl.BlockSpec(memory_space=pltpu.VMEM)
    token = pltpu.VMEM((tokens, D), BF16)
    tokens_of = lambda k: pltpu.VMEM((k, tokens, D), BF16)
    raw = pltpu.VMEM((frames, CELL, D), BF16)
    weight = pltpu.VMEM((D, D), BF16)
    dma = lambda k: pltpu.SemaphoreType.DMA((k,))
    array = lambda *dims: pltpu.VMEM(dims, BF16)
    total = 4 * devices * tokens
    windows = len(lane_chunks(D, WIN))
    result = pl.pallas_call(
        functools.partial(kernel, n, total),
        out_shape=[jax.ShapeDtypeStruct((tokens, D), BF16)] * 6
        + [jax.ShapeDtypeStruct((rows_z, D // 4), F32)] * 2,
        in_specs=[any_space] * 13 + [vmem] * 2,
        out_specs=[any_space] * 6 + [vmem] * 2,
        scratch_shapes=[token] * 3
        + [raw] * 3
        + [token]
        + [weight] * 2
        + [pltpu.VMEM(m.shape, BF16) for m in maps]
        + [pltpu.VMEM((D // 128, tokens, 128), F32), pltpu.VMEM((3 * WIN // 128, tokens, 128), F32)]
        + [token] * 3
        + [raw] * 2
        + [tokens_of(2)] * 2
        + [token]
        + [array(HEADS, tokens, tokens)] * 2
        + [tokens_of(3)] * 2
        + [array(devices, 3, CELL, D)] * 2
        + [token] * 2
        + [weight, array(D, D - split), array(D, split), array(D, D - split)]
        + [array(n * pad_y, split), array(n * pad_y, D - split)] * 2
        + [array(n, rows_z, D)] * 2
        + [array(rows_z, D)]
        + [array(rows_z, half)] * 3
        + [dma(13), dma(6), dma(6 + windows)]
        + [dma(1)] * 2
        + [dma(windows)] * 2
        + [dma(5 * n)] * 2
        + [dma(4)] * 2,
        compiler_params=pltpu.CompilerParams(
            collective_id=0, has_side_effects=True, vmem_limit_bytes=60 * 1024 * 1024
        ),
    )(flat(qs), flat(ks), flat(vs), cells(qt), cells(kt), cells(vt), flat(cot), ws, wt, *maps, gate_s, gate_t)
    return tuple(a.reshape(shape) for a in result[:6]) + tuple(result[6:])


def solution(mesh):
    n = round(mesh.shape["seq"] ** (1 / 3))
    maps = row_maps(n)
    frames = P("dp", "seq", None, None)
    cells = P("dp", None, "seq", None)

    def run(*args):
        return per_device(n, [jnp.asarray(m) for m in maps], *args)

    return jax.shard_map(
        run,
        mesh=mesh,
        in_specs=(frames,) * 3 + (cells,) * 3 + (frames, P("dp", None), P("dp", None), P(), P()),
        out_specs=(frames,) * 6 + (P("seq", "dp"),) * 2,
        check_vma=False,
    )
```

```python
import functools
import math

import jax
import jax.numpy as jnp
import numpy as np
from jax import lax
from jax.experimental import pallas as pl
from jax.experimental.pallas import tpu as pltpu
from jax.sharding import PartitionSpec as P

HEADS = 16
HEAD_DIM = 72
D = HEADS * HEAD_DIM
CELL = 4
WIN = 256
MESH = pl.DeviceIdType.MESH
F32 = jnp.float32
BF16 = jnp.bfloat16
CHUNK_HEADS = 5


def padded(rows):
    return -(-rows // 16) * 16


def row_maps(n):
    rows_x = D // n
    rows_y = rows_x // n
    rows_z = rows_y // n
    pad_y, pad_z = padded(rows_y), padded(rows_z)
    turn = np.zeros((D, D), np.float32)
    first_x = np.zeros((n * pad_y, D), np.float32)
    first_y = np.zeros((n * pad_y, D), np.float32)
    second = np.zeros((n * pad_z, n * pad_y), np.float32)
    r = np.arange(rows_z)
    for i in range(n):
        for zz in range(n):
            for j in range(n):
                turn[((j * n + i) * n + zz) * rows_z + r, ((i * n + zz) * n + j) * rows_z + r] = 1.0
                first_x[j * pad_y + zz * rows_z + r, i * rows_x + (zz * n + j) * rows_z + r] = 1.0
                first_y[j * pad_y + zz * rows_z + r, i * rows_x + (j * n + zz) * rows_z + r] = 1.0
            second[zz * pad_z + r, i * pad_y + zz * rows_z + r] = 1.0
    return [m.astype(jnp.bfloat16) for m in (turn, first_x, first_y, second)]


def dot(a, b):
    return lax.dot_general(a, b, (((1,), (0,)), ((), ())), preferred_element_type=F32)


def dot_rows(a, b):
    return lax.dot_general(a, b, (((0,), (0,)), ((), ())), preferred_element_type=F32)


def dot_lanes(a, b):
    return lax.dot_general(a, b, (((1,), (1,)), ((), ())), preferred_element_type=F32)


def head_mask(head, start, width):
    lane = lax.broadcasted_iota(jnp.int32, (1, width), 1) + start
    inside = (lane >= head * HEAD_DIM) & (lane < (head + 1) * HEAD_DIM)
    return jnp.where(inside, 1.0, 0.0).astype(BF16)


def lane_chunks(width, step):
    return [(start, min(step, width - start)) for start in range(0, width, step)]


def project(gated, weight, target, start, width):
    at = pl.ds(start, width)
    target[:, at] = dot_lanes(gated[...], weight[at, :]).astype(BF16)


def softmax_and_grad(scores, grads):
    factor = math.log2(math.e) / math.sqrt(HEAD_DIM)
    highest = jnp.max(scores, axis=0, keepdims=True)
    raised = jnp.exp2((scores - highest) * factor)
    shares = raised * (1.0 / jnp.sum(raised, axis=0, keepdims=True))
    centre = jnp.sum(shares * grads, axis=0, keepdims=True)
    return shares.astype(BF16), (shares * (grads - centre)).astype(BF16)


def window(head):
    start = jnp.minimum(head * HEAD_DIM // 128, (D - WIN) // 128) * 128
    return pl.multiple_of(start, 128)


def scores_space(q, k, v, u, shares, grads):
    def step(head, _):
        start = window(head)
        at = pl.ds(start, WIN)
        mask = head_mask(head, start, WIN)
        scores = dot_lanes(k[:, at] * mask, q[:, at])
        share_grad = dot_lanes(v[:, at] * mask, u[:, at])
        shares[head], grads[head] = softmax_and_grad(scores, share_grad)
        return 0

    lax.fori_loop(0, HEADS, step, 0, unroll=4)


def score_time(head, q, k, v, u, shares, grads):
    tokens = q.shape[0]
    half, frames = tokens // 2, tokens // CELL
    low = lax.broadcasted_iota(jnp.int32, (1, half), 1) < frames
    cell_of_lane = lax.broadcasted_iota(jnp.int32, (1, tokens), 1) // frames
    start = window(head)
    at = pl.ds(start, WIN)
    mask = head_mask(head, start, WIN)

    def compact(a, b):
        parts = []
        for i in range(2):
            rows = slice(i * half, (i + 1) * half)
            block = dot_lanes(a[rows, :], b[rows, :])
            parts.append(jnp.where(low, block[:frames, :], block[frames:, :]))
        return jnp.concatenate(parts, axis=1)

    def expand(block):
        zero = jnp.zeros_like(block)
        return jnp.concatenate([jnp.where(cell_of_lane == c, block, zero) for c in range(CELL)], axis=0)

    scores = compact(k[:, at] * mask, q[:, at])
    share_grad = compact(v[:, at] * mask, u[:, at])
    share, grad = softmax_and_grad(scores, share_grad)
    shares[head] = expand(share)
    grads[head] = expand(grad)


def gradients(first, heads, start, width, q, k, v, u, shares, grads, wanted=range(4)):
    at = pl.ds(start, width)
    totals = [None] * 4
    for i in range(heads):
        head = first + i
        mask = head_mask(head, start, width)
        for j in wanted:
            matrix = grads if j in (1, 2) else shares
            other = (v, k, q, u)[j]
            term = (dot_rows if j < 2 else dot)(matrix[head], other[:, at] * mask)
            totals[j] = term if totals[j] is None else totals[j] + term
    factor = 1.0 / math.sqrt(HEAD_DIM)
    return [totals[j] * factor if j in (1, 2) else totals[j] for j in wanted]


def to_slabs(source, target, count):
    def step(i, _):
        wide = source[pl.ds(pl.multiple_of(i * 16, 16), 16), :].astype(F32)
        for j in range(16 // CELL):
            target[i * (16 // CELL) + j] = wide[j * CELL : (j + 1) * CELL, :].astype(BF16)
        return 0

    lax.fori_loop(0, count * CELL // 16, step, 0, unroll=2)


def slabs_to_cells(source, wide):
    frames = source.shape[0]

    def step(f, _):
        slab = source[f].astype(F32)
        for t in range(D // 128):
            wide[t, pl.ds(f, CELL, stride=frames), :] = slab[:, t * 128 : (t + 1) * 128]
        return 0

    lax.fori_loop(0, frames, step, 0, unroll=8)


def kernel(
    n,
    tokens_total,
    qs_h,
    ks_h,
    vs_h,
    qt_h,
    kt_h,
    vt_h,
    cot_h,
    ws_h,
    wt_h,
    turn_h,
    first_x_h,
    first_y_h,
    second_h,
    gate_s,
    gate_t,
    dqs_o,
    dks_o,
    dvs_o,
    dqt_o,
    dkt_o,
    dvt_o,
    gws_o,
    gwt_o,
    qs,
    ks,
    vs,
    qraw,
    kraw,
    vraw,
    cot,
    ws,
    wt,
    turn,
    first_x,
    first_y,
    second,
    wide,
    parts,
    qt,
    kt,
    vt,
    cot_slabs,
    cot_got,
    gated,
    attended,
    up,
    shares,
    grads,
    spatial,
    temporal,
    sent,
    got,
    far_a,
    far_g,
    product,
    turned,
    got_1x,
    got_1y,
    send_2x,
    send_2y,
    got_2x,
    got_2y,
    send_z,
    got_z,
    load_sem,
    store_sem,
    own_sem,
    cot_send,
    cot_recv,
    t_send,
    t_recv,
    w_send,
    w_recv,
    z_send,
    z_recv,
    pair_send,
    pair_recv,
):
    dp = lax.axis_index("dp")
    seq = lax.axis_index("seq")
    devices = n * n * n
    group, y = seq // n, seq % n
    x, z = group // n, group % n
    side, core = dp // 2, dp % 2
    sibling = dp + 1 - 2 * core
    tokens = devices * CELL
    split, half = got_1x.shape[2], product.shape[2]
    half_step = D - half

    loads = [
        pltpu.make_async_copy(source, target, load_sem.at[i])
        for i, (source, target) in enumerate(
            (
                (cot_h, cot),
                (ws_h, ws),
                (qs_h, qs),
                (ks_h, ks),
                (vs_h, vs),
                (qt_h, qraw),
                (kt_h, kraw),
                (vt_h, vraw),
                (wt_h, wt),
                (turn_h, turn),
                (first_x_h, first_x),
                (first_y_h, first_y),
                (second_h, second),
            )
        )
    ]
    for load in loads:
        load.start()

    def seq_peer(s):
        return (dp, s)

    def y_peer(yy):
        return (dp, group * n + yy)

    def x_peer(xx):
        return (dp, (xx * n + z) * n + y)

    def column_peer(q):
        return (q // n, (x * n + q % n) * n + y)

    barrier = pltpu.get_barrier_semaphore()

    def greet(device):
        pl.semaphore_signal(barrier, inc=1, device_id=device, device_id_type=MESH)

    def greet_seq(i, _):
        greet(seq_peer((seq + i) % devices))
        return 0

    lax.fori_loop(1, devices, greet_seq, 0)
    for i in range(1, 4):
        for zz in range(n):
            greet(column_peer((dp + i) % 4 * n + zz))
    loads[0].wait()
    to_slabs(cot, cot_slabs, devices)
    pl.semaphore_wait(barrier, devices - 1 + 3 * n)

    def remote(source, target, send, recv, device):
        return pltpu.make_async_remote_copy(
            src_ref=source,
            dst_ref=target,
            send_sem=send,
            recv_sem=recv,
            device_id=device,
            device_id_type=MESH,
        )

    def local(source, target, sem):
        return pltpu.make_async_copy(source, target, sem)

    def send_cot(i, _):
        peer = (seq + i) % devices
        remote(cot_slabs.at[peer], cot_got.at[seq], cot_send.at[0], cot_recv.at[0], seq_peer(peer)).start()
        return 0

    lax.fori_loop(1, devices, send_cot, 0)
    cot_own = local(cot_slabs.at[seq], cot_got.at[seq], own_sem.at[0])
    cot_own.start()

    gated[0] = (gate_s[...] * cot[...].astype(F32)).astype(BF16)

    def pair_gated(kind):
        k = 2 * kind
        lanes = pl.ds(pl.multiple_of((1 - core) * half_step, 128), half)
        return remote(
            gated.at[kind, :, lanes], far_g.at[kind], pair_send.at[k], pair_recv.at[k], (sibling, seq)
        )

    pair_gated(0).start()
    loads[1].wait()
    for start, width in lane_chunks(D, 384):
        project(gated.at[0], ws, up, start, width)
    for load in loads[2:5]:
        load.wait()
    scores_space(qs, ks, vs, up, shares, grads)
    whole = D // WIN
    tail = whole * WIN

    def space_window(first, heads, start, width):
        at = pl.ds(start, width)
        total = gradients(first, heads, start, width, qs, ks, vs, up, shares, grads)
        attended[0, :, at] = total[0].astype(BF16)
        for i in range(3):
            spatial[i, :, at] = total[1 + i].astype(BF16)

    def space_step(i, _):
        start = pl.multiple_of(i * WIN, 128)
        space_window(start // HEAD_DIM, CHUNK_HEADS, start, WIN)
        return 0

    lax.fori_loop(0, whole, space_step, 0)
    space_window(tail // HEAD_DIM, HEADS - tail // HEAD_DIM, tail, D - tail)

    def pair_attended(kind, i, at):
        k = 2 * kind + i
        return remote(
            attended.at[kind, :, at], far_a.at[kind, :, at], pair_send.at[k], pair_recv.at[k], (sibling, seq)
        )

    pair_attended(0, 1, slice(0, D)).start()

    stores = [local(spatial.at[i], out, store_sem.at[i]) for i, out in enumerate((dqs_o, dks_o, dvs_o))]
    for store in stores:
        store.start()

    for raw, target, load in ((qraw, qt, loads[5]), (kraw, kt, loads[6]), (vraw, vt, loads[7])):
        load.wait()
        slabs_to_cells(raw, wide)
        for t in range(D // 128):
            target[:, t * 128 : (t + 1) * 128] = wide[t].astype(BF16)

    def rows(ref, at, count):
        return ref.at[pl.ds(pl.multiple_of(at * count, 16 if count % 16 == 0 else 8), count)]

    def exchange(me, device, source, target, slot, size=n):
        copies = []
        for i in range(1, size):
            peer = (me + i) % size
            k = slot * n + i
            copies.append(remote(source(peer), target(me), w_send.at[k], w_recv.at[k], device(peer)))
        own = local(source(me), target(me), own_sem.at[1 + slot])
        return own, copies

    count_1, count_2 = D // n, send_2x.shape[1] // n
    lanes_1 = slice(0, split)

    def all_steps(kind):
        k = 4 * kind
        return (
            exchange(
                x,
                x_peer,
                lambda p: rows(product.at[kind], p, count_1).at[:, lanes_1],
                lambda p: rows(got_1x.at[kind], p, count_1),
                k,
            ),
            exchange(
                y,
                y_peer,
                lambda p: rows(turned.at[kind], p, count_1),
                lambda p: rows(got_1y.at[kind], p, count_1),
                k + 1,
            ),
            exchange(
                y,
                y_peer,
                lambda p: rows(send_2x.at[kind], p, count_2),
                lambda p: rows(got_2x.at[kind], p, count_2),
                k + 2,
            ),
            exchange(
                x,
                x_peer,
                lambda p: rows(send_2y.at[kind], p, count_2),
                lambda p: rows(got_2y.at[kind], p, count_2),
                k + 3,
            ),
        )

    steps = (all_steps(0), all_steps(1))

    owners = 2 * n
    to_self = core == side

    def owner_part(kind, e):
        return send_z.at[kind, e % n, :, pl.ds(pl.multiple_of(e // n * 256, 128), 384)]

    def owner_copy(kind, e):
        place = side * n + z
        return remote(
            owner_part(kind, e),
            got_z.at[kind, place],
            z_send.at[kind * owners + e],
            z_recv.at[kind * owners + place],
            column_peer((2 * core + e // n) * n + e % n),
        )

    def owner_own(kind):
        return local(owner_part(kind, core * n + z), got_z.at[kind, side * n + z], own_sem.at[9 + kind])

    def owner_each(first, use_own, use):
        @pl.when(to_self)
        def _():
            use_own()

        @pl.when(jnp.logical_not(to_self))
        def _():
            use(first)

        for i in range(1, owners):
            use((first + i) % owners)

    def begin_z(kind):
        owner_each(core * n + z, lambda: owner_own(kind).start(), lambda e: owner_copy(kind, e).start())

    def sent_z(kind):
        owner_each(core * n + z, lambda: None, lambda e: owner_copy(kind, e).wait_send())

    def arrived_z(kind):
        def wait(s):
            place = got_z.at[kind, s]
            local(place, place, z_recv.at[kind * owners + s]).wait()

        owner_each(side * n + z, lambda: owner_own(kind).wait(), wait)

    def begin(step):
        own, copies = step
        for copy in copies:
            copy.start()
        own.start()

    def arrived(step):
        own, copies = step
        own.wait()
        for copy in copies:
            copy.wait_recv()

    scale = 1.0 / math.sqrt(tokens_total)

    def product_rows(kind, first, blocks):
        def step(i, _):
            at = pl.ds(pl.multiple_of((first + i) * 128, 128), 128)
            for start, width in lane_chunks(half, 384):
                to = slice(start, start + width)
                near = gated[kind, :, pl.ds(pl.multiple_of(core * half_step + start, 128), width)]
                total = dot_rows(attended[kind, :, at], near) + dot_rows(far_a[kind, :, at], far_g[kind, :, to])
                product[kind, at, to] = (total * scale).astype(BF16)
            return 0

        lax.fori_loop(0, blocks, step, 0, unroll=math.gcd(blocks, 3) if blocks > 2 else blocks)

    def turn_product(kind):
        def turn_rows(i, _):
            at = pl.ds(pl.multiple_of(i * 128, 128), 128)
            turned[kind, at, :] = dot(turn[at, :], product[kind, :, split:]).astype(BF16)
            return 0

        lax.fori_loop(0, D // 128, turn_rows, 0, unroll=3)
        begin(steps[kind][1])

    def weight_second(kind):
        for at, matrix, source, target in ((0, first_x, got_1x, send_2x), (1, first_y, got_1y, send_2y)):
            arrived(steps[kind][at])
            target[kind] = dot(matrix[...], source[kind]).astype(BF16)
            begin(steps[kind][2 + at])

    def weight_third(kind):
        pad, count = second.shape[0] // n, send_z.shape[2]
        for at, source, base in ((2, got_2x, 0), (3, got_2y, split)):
            arrived(steps[kind][at])
            total = dot(second[...], source[kind]).astype(BF16)
            for i in range(n):
                send_z[kind, i, :, base : base + total.shape[1]] = total[i * pad : i * pad + count, :]
        begin_z(kind)

    def weight_last(kind, out):
        arrived_z(kind)
        total = functools.reduce(lambda a, b: a + b, (got_z[kind, s].astype(F32) for s in range(owners)))
        width = out.shape[1]
        for i in range(4):

            @pl.when(dp == i)
            def _():
                base = i * width - i // 2 * half_step - i % 2 * 256
                out[...] = total[:, base : base + width]

    pair_gated(0).wait_recv()
    pair_attended(0, 1, slice(0, D)).wait_recv()
    product_rows(0, 0, D // 128)
    begin(steps[0][0])
    for load in loads[9:]:
        load.wait()
    turn_product(0)

    cot_own.wait()
    rest = pl.ds(0, devices - 1)
    local(cot_got.at[rest], cot_got.at[rest], cot_recv.at[0]).wait()
    slabs_to_cells(cot_got, wide)
    for t in range(D // 128):
        at = slice(t * 128, (t + 1) * 128)
        gated[1, :, at] = (gate_t[:, at] * wide[t]).astype(BF16)

    pair_gated(1).start()
    loads[8].wait()

    def time_attended(first, heads, start, width):
        at = pl.ds(start, width)
        (total,) = gradients(first, heads, start, width, qt, kt, vt, up, shares, grads, (0,))
        attended[1, :, at] = total.astype(BF16)

    def time_window(i, first, heads, start, width):
        at = pl.ds(start, width)
        total = gradients(first, heads, start, width, qt, kt, vt, up, shares, grads, (1, 2, 3))
        tiles = width // 128
        for t in range(3):
            for j in range(tiles):
                parts[t * tiles + j] = total[t][:, j * 128 : (j + 1) * 128]

        def narrow(f, _):
            for t in range(3):
                for j in range(tiles):
                    to = pl.ds(pl.multiple_of(start + j * 128, 128), 128)
                    sent[f, t, :, to] = parts[t * tiles + j, pl.ds(f, CELL, stride=devices), :].astype(BF16)
            return 0

        lax.fori_loop(0, devices, narrow, 0, unroll=8)

        def send(k, _):
            peer = (seq + k) % devices
            remote(
                sent.at[peer, :, :, at], got.at[seq, :, :, at], t_send.at[i], t_recv.at[i], seq_peer(peer)
            ).start()
            return 0

        lax.fori_loop(1, devices, send, 0)
        local(sent.at[seq, :, :, at], got.at[seq, :, :, at], own_sem.at[11 + i]).start()

    def time_scores(first, count):
        def step(i, _):
            score_time(first + i, qt, kt, vt, up, shares, grads)
            return 0

        lax.fori_loop(0, count, step, 0, unroll=4)

    def place_of(i):
        start = pl.multiple_of(i * WIN, 128)
        return start // HEAD_DIM, CHUNK_HEADS, start, WIN

    last = (tail // HEAD_DIM, HEADS - tail // HEAD_DIM, tail, D - tail)
    early = (slice(0, WIN), slice(WIN, D))

    project(gated.at[1], wt, up, 0, 384)
    time_scores(0, 4)
    time_attended(0, 4, 0, WIN)
    pair_attended(1, 1, early[0]).start()
    time_window(0, 0, 4, 0, WIN)

    for start, width in lane_chunks(D, 384)[1:]:
        project(gated.at[1], wt, up, start, width)
    time_scores(4, HEADS - 4)

    def attended_step(i, _):
        time_attended(*place_of(i))
        return 0

    lax.fori_loop(1, whole, attended_step, 0)
    time_attended(*last)
    pair_attended(1, 2, early[1]).start()
    time_window(1, *place_of(1))
    pair_gated(1).wait_recv()
    for i, at in enumerate(early):
        pair_attended(1, 1 + i, at).wait_recv()
    product_rows(1, 0, D // 128)
    begin(steps[1][0])
    turn_product(1)
    weight_second(0)

    def window_step(i, _):
        time_window(i, *place_of(i))
        return 0

    lax.fori_loop(2, whole, window_step, 0)
    time_window(whole, *last)
    weight_third(0)
    weight_second(1)
    weight_third(1)
    weight_last(0, gws_o)

    windows = lane_chunks(D, WIN)
    for i, (start, width) in enumerate(windows):
        at = slice(start, start + width)
        local(sent.at[seq, :, :, at], got.at[seq, :, :, at], own_sem.at[11 + i]).wait()
        piece = got.at[rest, :, :, at]
        local(piece, piece, t_recv.at[i]).wait()

        def join(k, _):
            for t in range(3):
                slabs = [got[k * (16 // CELL) + j, t, :, at].astype(F32) for j in range(16 // CELL)]
                to = pl.ds(pl.multiple_of(k * 16, 16), 16)
                temporal[t, to, at] = jnp.concatenate(slabs, axis=0).astype(BF16)
            return 0

        lax.fori_loop(0, tokens // 16, join, 0, unroll=2)
    final = [local(temporal.at[i], out, store_sem.at[3 + i]) for i, out in enumerate((dqt_o, dkt_o, dvt_o))]
    for store in final:
        store.start()

    weight_last(1, gwt_o)
    for store in stores + final:
        store.wait()
    local(cot_slabs.at[rest], cot_slabs.at[rest], cot_send.at[0]).wait()
    for i, (start, width) in enumerate(windows):
        piece = sent.at[rest, :, :, start : start + width]
        local(piece, piece, t_send.at[i]).wait()
    for kind in range(2):
        for _, copies in steps[kind]:
            for copy in copies:
                copy.wait_send()
        sent_z(kind)
        pair_gated(kind).wait_send()
    pair_attended(0, 1, slice(0, D)).wait_send()
    for i, at in enumerate(early):
        pair_attended(1, 1 + i, at).wait_send()


def hand_over(*refs):
    sources, targets, buffers, (in_sem, out_sem) = refs[:6], refs[6:12], refs[12:18], refs[18:]
    steps = [
        (pltpu.make_async_copy(s, b, in_sem.at[i]), pltpu.make_async_copy(b, t, out_sem.at[i]))
        for i, (s, b, t) in enumerate(zip(sources, buffers, targets))
    ]
    for come, _ in steps:
        come.start()
    for come, go in steps:
        come.wait()
        go.start()
    for _, go in steps:
        go.wait()


def per_device(n, maps, qs, ks, vs, qt, kt, vt, cot, gate_s, gate_t, ws, wt):
    tokens = cot.shape[2]
    frames = qt.shape[1]
    devices = n * n * n
    rows_z = D // devices
    pad_y = padded(D // n // n)
    split, half = 384, D // 2 + 64
    shape = cot.shape
    flat = lambda a: a.reshape(tokens, D)
    cells = lambda a: a.reshape(frames, CELL, D)
    any_space = pl.BlockSpec(memory_space=pl.ANY)
    vmem = pl.BlockSpec(memory_space=pltpu.VMEM)
    token = pltpu.VMEM((tokens, D), BF16)
    tokens_of = lambda k: pltpu.VMEM((k, tokens, D), BF16)
    raw = pltpu.VMEM((frames, CELL, D), BF16)
    weight = pltpu.VMEM((D, D), BF16)
    dma = lambda k: pltpu.SemaphoreType.DMA((k,))
    array = lambda *dims: pltpu.VMEM(dims, BF16)
    total = 4 * devices * tokens
    windows = len(lane_chunks(D, WIN))
    result = pl.pallas_call(
        functools.partial(kernel, n, total),
        out_shape=[jax.ShapeDtypeStruct((tokens, D), BF16)] * 6
        + [jax.ShapeDtypeStruct((rows_z, D // 4), F32)] * 2,
        in_specs=[any_space] * 13 + [vmem] * 2,
        out_specs=[any_space] * 6 + [vmem] * 2,
        scratch_shapes=[token] * 3
        + [raw] * 3
        + [token]
        + [weight] * 2
        + [pltpu.VMEM(m.shape, BF16) for m in maps]
        + [pltpu.VMEM((D // 128, tokens, 128), F32), pltpu.VMEM((3 * WIN // 128, tokens, 128), F32)]
        + [token] * 3
        + [raw] * 2
        + [tokens_of(2)] * 2
        + [token]
        + [array(HEADS, tokens, tokens)] * 2
        + [tokens_of(3)] * 2
        + [array(devices, 3, CELL, D)] * 2
        + [tokens_of(2), array(2, tokens, half)]
        + [array(2, D, half), array(2, D, half - split), array(2, D, split), array(2, D, half - split)]
        + [array(2, n * pad_y, split), array(2, n * pad_y, half - split)] * 2
        + [array(2, n, rows_z, half), array(2, 2 * n, rows_z, 384)]
        + [dma(13), dma(6), dma(11 + windows)]
        + [dma(1)] * 2
        + [dma(windows)] * 2
        + [dma(8 * n)] * 2
        + [dma(4 * n)] * 2
        + [dma(5)] * 2,
        compiler_params=pltpu.CompilerParams(
            collective_id=0, has_side_effects=True, vmem_limit_bytes=60 * 1024 * 1024
        ),
    )(flat(qs), flat(ks), flat(vs), cells(qt), cells(kt), cells(vt), flat(cot), ws, wt, *maps, gate_s, gate_t)
    tensors = pl.pallas_call(
        hand_over,
        out_shape=[jax.ShapeDtypeStruct((tokens, D), BF16)] * 6,
        in_specs=[any_space] * 6,
        out_specs=[any_space] * 6,
        scratch_shapes=[token] * 6 + [dma(6)] * 2,
    )(*result[:6])
    return tuple(a.reshape(shape) for a in tensors) + tuple(result[6:])


def solution(mesh):
    n = round(mesh.shape["seq"] ** (1 / 3))
    maps = row_maps(n)
    frames = P("dp", "seq", None, None)
    cells = P("dp", None, "seq", None)

    def run(*args):
        return per_device(n, [jnp.asarray(m) for m in maps], *args)

    return jax.shard_map(
        run,
        mesh=mesh,
        in_specs=(frames,) * 3 + (cells,) * 3 + (frames, P("dp", None), P("dp", None), P(), P()),
        out_specs=(frames,) * 6 + (P("seq", "dp"),) * 2,
        check_vma=False,
    )
```

```python
import functools
import math

import jax
import jax.numpy as jnp
import numpy as np
from jax import lax
from jax.experimental import pallas as pl
from jax.experimental.pallas import tpu as pltpu
from jax.sharding import PartitionSpec as P

HEADS = 16
HEAD_DIM = 72
D = HEADS * HEAD_DIM
CELL = 4
WIN = 256
FIRST = 128
MESH = pl.DeviceIdType.MESH
F32 = jnp.float32
BF16 = jnp.bfloat16
CHUNK_HEADS = 5


def padded(rows):
    return -(-rows // 16) * 16


def row_maps(n):
    rows_x = D // n
    rows_y = rows_x // n
    rows_z = rows_y // n
    pad_y, pad_z = padded(rows_y), padded(rows_z)
    turn = np.zeros((D, D), np.float32)
    first_x = np.zeros((n * pad_y, D), np.float32)
    first_y = np.zeros((n * pad_y, D), np.float32)
    second = np.zeros((n * pad_z, n * pad_y), np.float32)
    r = np.arange(rows_z)
    for i in range(n):
        for zz in range(n):
            for j in range(n):
                turn[((j * n + i) * n + zz) * rows_z + r, ((i * n + zz) * n + j) * rows_z + r] = 1.0
                first_x[j * pad_y + zz * rows_z + r, i * rows_x + (zz * n + j) * rows_z + r] = 1.0
                first_y[j * pad_y + zz * rows_z + r, i * rows_x + (j * n + zz) * rows_z + r] = 1.0
            second[zz * pad_z + r, i * pad_y + zz * rows_z + r] = 1.0
    return [m.astype(jnp.bfloat16) for m in (turn, first_x, first_y, second)]


def dot(a, b):
    return lax.dot_general(a, b, (((1,), (0,)), ((), ())), preferred_element_type=F32)


def dot_rows(a, b):
    return lax.dot_general(a, b, (((0,), (0,)), ((), ())), preferred_element_type=F32)


def dot_lanes(a, b):
    return lax.dot_general(a, b, (((1,), (1,)), ((), ())), preferred_element_type=F32)


def head_mask(head, start, width):
    lane = lax.broadcasted_iota(jnp.int32, (1, width), 1) + start
    inside = (lane >= head * HEAD_DIM) & (lane < (head + 1) * HEAD_DIM)
    return jnp.where(inside, 1.0, 0.0).astype(BF16)


def lane_chunks(width, step):
    return [(start, min(step, width - start)) for start in range(0, width, step)]


def project(gated, weight, target, start, width):
    at = pl.ds(start, width)
    target[:, at] = dot_lanes(gated[...], weight[at, :]).astype(BF16)


def softmax_and_grad(scores, grads):
    factor = math.log2(math.e) / math.sqrt(HEAD_DIM)
    highest = jnp.max(scores, axis=0, keepdims=True)
    raised = jnp.exp2((scores - highest) * factor)
    shares = raised * (1.0 / jnp.sum(raised, axis=0, keepdims=True))
    centre = jnp.sum(shares * grads, axis=0, keepdims=True)
    return shares.astype(BF16), (shares * (grads - centre)).astype(BF16)


def window(head):
    start = jnp.minimum(head * HEAD_DIM // 128, (D - WIN) // 128) * 128
    return pl.multiple_of(start, 128)


def scores_space(q, k, v, u, shares, grads):
    def step(head, _):
        start = window(head)
        at = pl.ds(start, WIN)
        mask = head_mask(head, start, WIN)
        scores = dot_lanes(k[:, at] * mask, q[:, at])
        share_grad = dot_lanes(v[:, at] * mask, u[:, at])
        shares[head], grads[head] = softmax_and_grad(scores, share_grad)
        return 0

    lax.fori_loop(0, HEADS, step, 0, unroll=4)


def score_time(head, q, k, v, u, shares, grads):
    tokens = q.shape[0]
    half, frames = tokens // 2, tokens // CELL
    low = lax.broadcasted_iota(jnp.int32, (1, half), 1) < frames
    cell_of_lane = lax.broadcasted_iota(jnp.int32, (1, tokens), 1) // frames
    start = window(head)
    at = pl.ds(start, WIN)
    mask = head_mask(head, start, WIN)

    def compact(a, b):
        parts = []
        for i in range(2):
            rows = slice(i * half, (i + 1) * half)
            block = dot_lanes(a[rows, :], b[rows, :])
            parts.append(jnp.where(low, block[:frames, :], block[frames:, :]))
        return jnp.concatenate(parts, axis=1)

    def expand(block):
        zero = jnp.zeros_like(block)
        return jnp.concatenate([jnp.where(cell_of_lane == c, block, zero) for c in range(CELL)], axis=0)

    scores = compact(k[:, at] * mask, q[:, at])
    share_grad = compact(v[:, at] * mask, u[:, at])
    share, grad = softmax_and_grad(scores, share_grad)
    shares[head] = expand(share)
    grads[head] = expand(grad)


def gradients(first, heads, start, width, q, k, v, u, shares, grads, wanted=range(4)):
    at = pl.ds(start, width)
    totals = [None] * 4
    for i in range(heads):
        head = first + i
        mask = head_mask(head, start, width)
        for j in wanted:
            matrix = grads if j in (1, 2) else shares
            other = (v, k, q, u)[j]
            term = (dot_rows if j < 2 else dot)(matrix[head], other[:, at] * mask)
            totals[j] = term if totals[j] is None else totals[j] + term
    factor = 1.0 / math.sqrt(HEAD_DIM)
    return [totals[j] * factor if j in (1, 2) else totals[j] for j in wanted]


def to_slabs(source, target, count):
    def step(i, _):
        wide = source[pl.ds(pl.multiple_of(i * 16, 16), 16), :].astype(F32)
        for j in range(16 // CELL):
            target[i * (16 // CELL) + j] = wide[j * CELL : (j + 1) * CELL, :].astype(BF16)
        return 0

    lax.fori_loop(0, count * CELL // 16, step, 0, unroll=2)


def slabs_to_cells(source, wide):
    frames = source.shape[0]

    def step(f, _):
        slab = source[f].astype(F32)
        for t in range(D // 128):
            wide[t, pl.ds(f, CELL, stride=frames), :] = slab[:, t * 128 : (t + 1) * 128]
        return 0

    lax.fori_loop(0, frames, step, 0, unroll=8)


def kernel(
    n,
    tokens_total,
    qs_h,
    ks_h,
    vs_h,
    qt_h,
    kt_h,
    vt_h,
    cot_h,
    ws_h,
    wt_h,
    turn_h,
    first_x_h,
    first_y_h,
    second_h,
    gate_s,
    gate_t,
    dqs_o,
    dks_o,
    dvs_o,
    dqt_o,
    dkt_o,
    dvt_o,
    gws_o,
    gwt_o,
    qs,
    ks,
    vs,
    qraw,
    kraw,
    vraw,
    cot,
    ws,
    wt,
    turn,
    first_x,
    first_y,
    second,
    wide,
    parts,
    qt,
    kt,
    vt,
    cot_slabs,
    cot_got,
    gated,
    attended,
    up,
    shares,
    grads,
    spatial,
    temporal,
    sent_0,
    got_0,
    sent,
    got,
    far_a,
    far_g,
    product,
    turned,
    got_1x,
    got_1y,
    send_2x,
    send_2y,
    got_2x,
    got_2y,
    send_z,
    got_z,
    load_sem,
    store_sem,
    own_sem,
    cot_send,
    cot_recv,
    t_send,
    t_recv,
    w_send,
    w_recv,
    z_send,
    z_recv,
    pair_send,
    pair_recv,
):
    dp = lax.axis_index("dp")
    seq = lax.axis_index("seq")
    devices = n * n * n
    group, y = seq // n, seq % n
    x, z = group // n, group % n
    side, core = dp // 2, dp % 2
    sibling = dp + 1 - 2 * core
    tokens = devices * CELL
    split, half = got_1x.shape[2], product.shape[2]
    half_step = D - half

    loads = [
        pltpu.make_async_copy(source, target, load_sem.at[i])
        for i, (source, target) in enumerate(
            (
                (cot_h, cot),
                (ws_h, ws),
                (qs_h, qs),
                (ks_h, ks),
                (vs_h, vs),
                (qt_h, qraw),
                (kt_h, kraw),
                (vt_h, vraw),
                (wt_h, wt),
                (turn_h, turn),
                (first_x_h, first_x),
                (first_y_h, first_y),
                (second_h, second),
            )
        )
    ]
    for load in loads:
        load.start()

    def seq_peer(s):
        return (dp, s)

    def y_peer(yy):
        return (dp, group * n + yy)

    def x_peer(xx):
        return (dp, (xx * n + z) * n + y)

    def column_peer(q):
        return (q // n, (x * n + q % n) * n + y)

    barrier = pltpu.get_barrier_semaphore()

    def greet(device):
        pl.semaphore_signal(barrier, inc=1, device_id=device, device_id_type=MESH)

    def greet_seq(i, _):
        greet(seq_peer((seq + i) % devices))
        return 0

    lax.fori_loop(1, devices, greet_seq, 0)
    for i in range(1, 4):
        for zz in range(n):
            greet(column_peer((dp + i) % 4 * n + zz))
    loads[0].wait()
    to_slabs(cot, cot_slabs, devices)
    pl.semaphore_wait(barrier, devices - 1 + 3 * n)

    def remote(source, target, send, recv, device):
        return pltpu.make_async_remote_copy(
            src_ref=source,
            dst_ref=target,
            send_sem=send,
            recv_sem=recv,
            device_id=device,
            device_id_type=MESH,
        )

    def local(source, target, sem):
        return pltpu.make_async_copy(source, target, sem)

    def send_cot(i, _):
        peer = (seq + i) % devices
        remote(cot_slabs.at[peer], cot_got.at[seq], cot_send.at[0], cot_recv.at[0], seq_peer(peer)).start()
        return 0

    lax.fori_loop(1, devices, send_cot, 0)
    cot_own = local(cot_slabs.at[seq], cot_got.at[seq], own_sem.at[0])
    cot_own.start()

    gated[0] = (gate_s[...] * cot[...].astype(F32)).astype(BF16)

    def pair_gated(kind):
        k = 2 * kind
        lanes = pl.ds(pl.multiple_of((1 - core) * half_step, 128), half)
        return remote(
            gated.at[kind, :, lanes], far_g.at[kind], pair_send.at[k], pair_recv.at[k], (sibling, seq)
        )

    pair_gated(0).start()
    loads[1].wait()
    for start, width in lane_chunks(D, 384):
        project(gated.at[0], ws, up.at[0], start, width)
    for load in loads[2:5]:
        load.wait()
    space = (qs, ks, vs, up.at[0], shares.at[0], grads.at[0])
    scores_space(*space)
    whole = D // WIN
    tail = whole * WIN

    def space_attended(first, heads, start, width):
        (total,) = gradients(first, heads, start, width, *space, (0,))
        attended[0, :, pl.ds(start, width)] = total.astype(BF16)

    def space_window(first, heads, start, width):
        total = gradients(first, heads, start, width, *space, (1, 2, 3))
        for i in range(3):
            spatial[i, :, pl.ds(start, width)] = total[i].astype(BF16)

    def space_windows(window_of):
        def step(i, _):
            start = pl.multiple_of(i * WIN, 128)
            window_of(start // HEAD_DIM, CHUNK_HEADS, start, WIN)
            return 0

        lax.fori_loop(0, whole, step, 0)
        window_of(tail // HEAD_DIM, HEADS - tail // HEAD_DIM, tail, D - tail)

    space_windows(space_attended)

    def pair_attended(kind, i, at):
        k = 2 * kind + i
        return remote(
            attended.at[kind, :, at], far_a.at[kind, :, at], pair_send.at[k], pair_recv.at[k], (sibling, seq)
        )

    pair_attended(0, 1, slice(0, D)).start()

    for raw, target, load in ((qraw, qt, loads[5]), (kraw, kt, loads[6]), (vraw, vt, loads[7])):
        load.wait()
        slabs_to_cells(raw, wide)
        for t in range(D // 128):
            target[:, t * 128 : (t + 1) * 128] = wide[t].astype(BF16)

    def rows(ref, at, count):
        return ref.at[pl.ds(pl.multiple_of(at * count, 16 if count % 16 == 0 else 8), count)]

    def exchange(me, device, source, target, slot, size=n):
        copies = []
        for i in range(1, size):
            peer = (me + i) % size
            k = slot * n + i
            copies.append(remote(source(peer), target(me), w_send.at[k], w_recv.at[k], device(peer)))
        own = local(source(me), target(me), own_sem.at[1 + slot])
        return own, copies

    count_1, count_2 = D // n, send_2x.shape[1] // n
    lanes_1 = slice(0, split)

    def all_steps(kind):
        k = 4 * kind
        return (
            exchange(
                x,
                x_peer,
                lambda p: rows(product.at[kind], p, count_1).at[:, lanes_1],
                lambda p: rows(got_1x.at[kind], p, count_1),
                k,
            ),
            exchange(
                y,
                y_peer,
                lambda p: rows(turned.at[kind], p, count_1),
                lambda p: rows(got_1y.at[kind], p, count_1),
                k + 1,
            ),
            exchange(
                y,
                y_peer,
                lambda p: rows(send_2x.at[kind], p, count_2),
                lambda p: rows(got_2x.at[kind], p, count_2),
                k + 2,
            ),
            exchange(
                x,
                x_peer,
                lambda p: rows(send_2y.at[kind], p, count_2),
                lambda p: rows(got_2y.at[kind], p, count_2),
                k + 3,
            ),
        )

    steps = (all_steps(0), all_steps(1))

    owners = 2 * n
    to_self = core == side

    def owner_part(kind, e):
        return send_z.at[kind, e % n, :, :, pl.ds(pl.multiple_of(e // n * 256, 128), 384)]

    def owner_copy(kind, e):
        place = side * n + z
        return remote(
            owner_part(kind, e),
            got_z.at[kind, place],
            z_send.at[kind * owners + e],
            z_recv.at[kind * owners + place],
            column_peer((2 * core + e // n) * n + e % n),
        )

    def owner_own(kind):
        return local(owner_part(kind, core * n + z), got_z.at[kind, side * n + z], own_sem.at[9 + kind])

    def owner_each(first, use_own, use):
        @pl.when(to_self)
        def _():
            use_own()

        @pl.when(jnp.logical_not(to_self))
        def _():
            use(first)

        for i in range(1, owners):
            use((first + i) % owners)

    def begin_z(kind):
        owner_each(core * n + z, lambda: owner_own(kind).start(), lambda e: owner_copy(kind, e).start())

    def sent_z(kind):
        owner_each(core * n + z, lambda: None, lambda e: owner_copy(kind, e).wait_send())

    def arrived_z(kind):
        def wait(s):
            place = got_z.at[kind, s]
            local(place, place, z_recv.at[kind * owners + s]).wait()

        owner_each(side * n + z, lambda: owner_own(kind).wait(), wait)

    def begin(step):
        own, copies = step
        for copy in copies:
            copy.start()
        own.start()

    def arrived(step):
        own, copies = step
        own.wait()
        for copy in copies:
            copy.wait_recv()

    scale = 1.0 / math.sqrt(tokens_total)

    def product_rows(kind, first, blocks):
        def step(i, _):
            at = pl.ds(pl.multiple_of((first + i) * 128, 128), 128)
            for start, width in lane_chunks(half, 384):
                to = slice(start, start + width)
                near = gated[kind, :, pl.ds(pl.multiple_of(core * half_step + start, 128), width)]
                total = dot_rows(attended[kind, :, at], near) + dot_rows(far_a[kind, :, at], far_g[kind, :, to])
                product[kind, at, to] = (total * scale).astype(BF16)
            return 0

        lax.fori_loop(0, blocks, step, 0, unroll=math.gcd(blocks, 3) if blocks > 2 else blocks)

    def turn_product(kind):
        def turn_rows(i, _):
            at = pl.ds(pl.multiple_of(i * 128, 128), 128)
            turned[kind, at, :] = dot(turn[at, :], product[kind, :, split:]).astype(BF16)
            return 0

        lax.fori_loop(0, D // 128, turn_rows, 0, unroll=3)
        begin(steps[kind][1])

    def weight_second(kind):
        for at, matrix, source, target in ((0, first_x, got_1x, send_2x), (1, first_y, got_1y, send_2y)):
            arrived(steps[kind][at])
            target[kind] = dot(matrix[...], source[kind]).astype(BF16)
            begin(steps[kind][2 + at])

    def weight_third(kind):
        pad, count = second.shape[0] // n, send_z.shape[2]
        for at, source, base in ((2, got_2x, 0), (3, got_2y, split)):
            arrived(steps[kind][at])
            total = dot(second[...], source[kind]).astype(BF16)
            for i in range(n):
                for j in range(count):
                    row = i * pad + 2 * j
                    send_z[kind, i, j, :, base : base + total.shape[1]] = total[row : row + 2, :]
        begin_z(kind)

    def weight_last(kind, out):
        arrived_z(kind)
        total = functools.reduce(lambda a, b: a + b, (got_z[kind, s].astype(F32) for s in range(owners)))
        total = jnp.concatenate([total[j] for j in range(total.shape[0])], axis=0)
        width = out.shape[1]
        for i in range(4):

            @pl.when(dp == i)
            def _():
                base = i * width - i // 2 * half_step - i % 2 * 256
                out[...] = total[:, base : base + width]

    pair_gated(0).wait_recv()
    pair_attended(0, 1, slice(0, D)).wait_recv()
    product_rows(0, 0, D // 128)
    begin(steps[0][0])
    for load in loads[9:]:
        load.wait()
    turn_product(0)

    cot_own.wait()
    rest = pl.ds(0, devices - 1)
    local(cot_got.at[rest], cot_got.at[rest], cot_recv.at[0]).wait()
    slabs_to_cells(cot_got, wide)
    for t in range(D // 128):
        at = slice(t * 128, (t + 1) * 128)
        gated[1, :, at] = (gate_t[:, at] * wide[t]).astype(BF16)

    pair_gated(1).start()
    loads[8].wait()

    time = (qt, kt, vt, up.at[1], shares.at[1], grads.at[1])

    def time_attended(first, heads, start, width):
        at = pl.ds(start, width)
        (total,) = gradients(first, heads, start, width, *time, (0,))
        attended[1, :, at] = total.astype(BF16)

    def pieces(i, width):
        return (sent_0, got_0) if width == FIRST else (sent.at[i - 1], got.at[i - 1])

    def time_window(i, first, heads, start, width):
        total = gradients(first, heads, start, width, *time, (1, 2, 3))
        tiles = width // 128
        out, come = pieces(i, width)
        for t in range(3):
            for j in range(tiles):
                parts[t * tiles + j] = total[t][:, j * 128 : (j + 1) * 128]

        def narrow(f, _):
            for t in range(3):
                for j in range(tiles):
                    slab = parts[t * tiles + j, pl.ds(f, CELL, stride=devices), :]
                    out[f, t, :, j * 128 : (j + 1) * 128] = slab.astype(BF16)
            return 0

        lax.fori_loop(0, devices, narrow, 0, unroll=8)

        def send(k, _):
            peer = (seq + k) % devices
            remote(out.at[peer], come.at[seq], t_send.at[i], t_recv.at[i], seq_peer(peer)).start()
            return 0

        lax.fori_loop(1, devices, send, 0)
        local(out.at[seq], come.at[seq], own_sem.at[11 + i]).start()

    def time_scores(first, count):
        def step(i, _):
            score_time(first + i, *time)
            return 0

        lax.fori_loop(0, count, step, 0, unroll=count if count < 5 else count // 2)

    def place_of(i):
        start = pl.multiple_of((i - 1) * WIN + FIRST, 128)
        return jnp.minimum(start // HEAD_DIM, HEADS - CHUNK_HEADS), CHUNK_HEADS, start, WIN

    opening = (0, -(-FIRST // HEAD_DIM), 0, FIRST)
    early = (slice(0, FIRST), slice(FIRST, D))

    project(gated.at[1], wt, up.at[1], 0, 256)
    time_scores(0, opening[1])
    time_window(0, *opening)

    project(gated.at[1], wt, up.at[1], 256, 512)
    time_scores(opening[1], CHUNK_HEADS + 1 - opening[1])
    time_window(1, *place_of(1))

    project(gated.at[1], wt, up.at[1], 768, 384)
    time_scores(CHUNK_HEADS + 1, HEADS - CHUNK_HEADS - 1)
    time_attended(*opening)
    pair_attended(1, 1, early[0]).start()

    def attended_step(i, _):
        time_attended(*place_of(i))
        return 0

    lax.fori_loop(1, whole + 1, attended_step, 0)
    pair_attended(1, 2, early[1]).start()
    pair_gated(1).wait_recv()
    for i, at in enumerate(early):
        pair_attended(1, 1 + i, at).wait_recv()
    product_rows(1, 0, D // 128)
    begin(steps[1][0])
    turn_product(1)
    weight_second(0)

    def window_step(i, _):
        time_window(i, *place_of(i))
        return 0

    lax.fori_loop(2, whole + 1, window_step, 0)
    space_windows(space_window)
    space_stores = [local(spatial.at[i], out, store_sem.at[i]) for i, out in enumerate((dqs_o, dks_o, dvs_o))]
    for store in space_stores:
        store.start()
    weight_third(0)
    weight_second(1)
    weight_third(1)
    weight_last(0, gws_o)

    outs = (dqt_o, dkt_o, dvt_o)
    stores = [(temporal.at[i], out) for i, out in enumerate(outs)]
    final = []
    for i in range(whole + 1):
        start, width = (0, FIRST) if i == 0 else ((i - 1) * WIN + FIRST, WIN)
        at = slice(start, start + width)
        out, come = pieces(i, width)
        local(out.at[seq], come.at[seq], own_sem.at[11 + i]).wait()
        local(come.at[rest], come.at[rest], t_recv.at[i]).wait()

        def join(k, _):
            for t in range(3):
                slabs = [come[k * (16 // CELL) + j, t].astype(F32) for j in range(16 // CELL)]
                to = pl.ds(pl.multiple_of(k * 16, 16), 16)
                temporal[t, to, at] = jnp.concatenate(slabs, axis=0).astype(BF16)
            return 0

        lax.fori_loop(0, tokens // 16, join, 0, unroll=2)
        for t, (source, target) in enumerate(stores):
            final.append(local(source.at[:, at], target.at[:, at], store_sem.at[3 + 3 * i + t]))
            final[-1].start()

    weight_last(1, gwt_o)
    for store in space_stores + final:
        store.wait()
    local(cot_slabs.at[rest], cot_slabs.at[rest], cot_send.at[0]).wait()
    for i in range(whole + 1):
        out, _ = pieces(i, FIRST if i == 0 else WIN)
        local(out.at[rest], out.at[rest], t_send.at[i]).wait()
    for kind in range(2):
        for _, copies in steps[kind]:
            for copy in copies:
                copy.wait_send()
        sent_z(kind)
        pair_gated(kind).wait_send()
    pair_attended(0, 1, slice(0, D)).wait_send()
    for i, at in enumerate(early):
        pair_attended(1, 1 + i, at).wait_send()


def hand_over(*refs):
    sources, targets, buffers, (in_sem, out_sem) = refs[:6], refs[6:12], refs[12:18], refs[18:]
    steps = [
        (pltpu.make_async_copy(s, b, in_sem.at[i]), pltpu.make_async_copy(b, t, out_sem.at[i]))
        for i, (s, b, t) in enumerate(zip(sources, buffers, targets))
    ]
    for come, _ in steps:
        come.start()
    for come, go in steps:
        come.wait()
        go.start()
    for _, go in steps:
        go.wait()


def per_device(n, maps, qs, ks, vs, qt, kt, vt, cot, gate_s, gate_t, ws, wt):
    tokens = cot.shape[2]
    frames = qt.shape[1]
    devices = n * n * n
    rows_z = D // devices
    pad_y = padded(D // n // n)
    split, half = 384, D // 2 + 64
    shape = cot.shape
    flat = lambda a: a.reshape(tokens, D)
    cells = lambda a: a.reshape(frames, CELL, D)
    any_space = pl.BlockSpec(memory_space=pl.ANY)
    vmem = pl.BlockSpec(memory_space=pltpu.VMEM)
    token = pltpu.VMEM((tokens, D), BF16)
    tokens_of = lambda k: pltpu.VMEM((k, tokens, D), BF16)
    raw = pltpu.VMEM((frames, CELL, D), BF16)
    weight = pltpu.VMEM((D, D), BF16)
    dma = lambda k: pltpu.SemaphoreType.DMA((k,))
    array = lambda *dims: pltpu.VMEM(dims, BF16)
    total = 4 * devices * tokens
    windows = 1 + (D - FIRST) // WIN
    result = pl.pallas_call(
        functools.partial(kernel, n, total),
        out_shape=[jax.ShapeDtypeStruct((tokens, D), BF16)] * 6
        + [jax.ShapeDtypeStruct((rows_z, D // 4), F32)] * 2,
        in_specs=[any_space] * 13 + [vmem] * 2,
        out_specs=[any_space] * 6 + [vmem] * 2,
        scratch_shapes=[token] * 3
        + [raw] * 3
        + [token]
        + [weight] * 2
        + [pltpu.VMEM(m.shape, BF16) for m in maps]
        + [pltpu.VMEM((D // 128, tokens, 128), F32), pltpu.VMEM((3 * WIN // 128, tokens, 128), F32)]
        + [token] * 3
        + [raw] * 2
        + [tokens_of(2)] * 2
        + [tokens_of(2)]
        + [array(2, HEADS, tokens, tokens)] * 2
        + [tokens_of(3)] * 2
        + [array(devices, 3, CELL, FIRST)] * 2
        + [array(windows - 1, devices, 3, CELL, WIN)] * 2
        + [tokens_of(2), array(2, tokens, half)]
        + [array(2, D, half), array(2, D, half - split), array(2, D, split), array(2, D, half - split)]
        + [array(2, n * pad_y, split), array(2, n * pad_y, half - split)] * 2
        + [array(2, n, rows_z // 2, 2, half), array(2, 2 * n, rows_z // 2, 2, 384)]
        + [dma(13), dma(3 + 3 * windows), dma(11 + windows)]
        + [dma(1)] * 2
        + [dma(windows)] * 2
        + [dma(8 * n)] * 2
        + [dma(4 * n)] * 2
        + [dma(5)] * 2,
        compiler_params=pltpu.CompilerParams(
            collective_id=0, has_side_effects=True, vmem_limit_bytes=60 * 1024 * 1024
        ),
    )(flat(qs), flat(ks), flat(vs), cells(qt), cells(kt), cells(vt), flat(cot), ws, wt, *maps, gate_s, gate_t)
    tensors = pl.pallas_call(
        hand_over,
        out_shape=[jax.ShapeDtypeStruct((tokens, D), BF16)] * 6,
        in_specs=[any_space] * 6,
        out_specs=[any_space] * 6,
        scratch_shapes=[token] * 6 + [dma(6)] * 2,
    )(*result[:6])
    return tuple(a.reshape(shape) for a in tensors) + tuple(result[6:])


def solution(mesh):
    n = round(mesh.shape["seq"] ** (1 / 3))
    maps = row_maps(n)
    frames = P("dp", "seq", None, None)
    cells = P("dp", None, "seq", None)

    def run(*args):
        return per_device(n, [jnp.asarray(m) for m in maps], *args)

    return jax.shard_map(
        run,
        mesh=mesh,
        in_specs=(frames,) * 3 + (cells,) * 3 + (frames, P("dp", None), P("dp", None), P(), P()),
        out_specs=(frames,) * 6 + (P("seq", "dp"),) * 2,
        check_vma=False,
    )
```

```python
import functools
import math

import jax
import jax.numpy as jnp
import numpy as np
from jax import lax
from jax.experimental import pallas as pl
from jax.experimental.pallas import tpu as pltpu
from jax.sharding import PartitionSpec as P

HEADS = 16
HEAD_DIM = 72
D = HEADS * HEAD_DIM
CELL = 4
WIN = 256
FIRST = 128
MESH = pl.DeviceIdType.MESH
F32 = jnp.float32
BF16 = jnp.bfloat16
CHUNK_HEADS = 5


def padded(rows):
    return -(-rows // 16) * 16


def row_maps(n):
    rows_x = D // n
    rows_y = rows_x // n
    rows_z = rows_y // n
    pad_y, pad_z = padded(rows_y), padded(rows_z)
    turn = np.zeros((D, D), np.float32)
    first_x = np.zeros((n * pad_y, D), np.float32)
    first_y = np.zeros((n * pad_y, D), np.float32)
    second = np.zeros((n * pad_z, n * pad_y), np.float32)
    r = np.arange(rows_z)
    for i in range(n):
        for zz in range(n):
            for j in range(n):
                turn[((j * n + i) * n + zz) * rows_z + r, ((i * n + zz) * n + j) * rows_z + r] = 1.0
                first_x[j * pad_y + zz * rows_z + r, i * rows_x + (zz * n + j) * rows_z + r] = 1.0
                first_y[j * pad_y + zz * rows_z + r, i * rows_x + (j * n + zz) * rows_z + r] = 1.0
            second[zz * pad_z + r, i * pad_y + zz * rows_z + r] = 1.0
    return [m.astype(jnp.bfloat16) for m in (turn, first_x, first_y, second)]


def dot(a, b):
    return lax.dot_general(a, b, (((1,), (0,)), ((), ())), preferred_element_type=F32)


def dot_rows(a, b):
    return lax.dot_general(a, b, (((0,), (0,)), ((), ())), preferred_element_type=F32)


def dot_lanes(a, b):
    return lax.dot_general(a, b, (((1,), (1,)), ((), ())), preferred_element_type=F32)


def head_mask(head, start, width):
    lane = lax.broadcasted_iota(jnp.int32, (1, width), 1) + start
    inside = (lane >= head * HEAD_DIM) & (lane < (head + 1) * HEAD_DIM)
    return jnp.where(inside, 1.0, 0.0).astype(BF16)


def lane_chunks(width, step):
    return [(start, min(step, width - start)) for start in range(0, width, step)]


def project(gated, weight, target, start, width):
    at = pl.ds(start, width)
    target[:, at] = dot_lanes(gated[...], weight[at, :]).astype(BF16)


def softmax_and_grad(scores, grads):
    factor = math.log2(math.e) / math.sqrt(HEAD_DIM)
    highest = jnp.max(scores, axis=0, keepdims=True)
    raised = jnp.exp2((scores - highest) * factor)
    shares = raised * (1.0 / jnp.sum(raised, axis=0, keepdims=True))
    centre = jnp.sum(shares * grads, axis=0, keepdims=True)
    return shares.astype(BF16), (shares * (grads - centre)).astype(BF16)


def window(head):
    start = jnp.minimum(head * HEAD_DIM // 128, (D - WIN) // 128) * 128
    return pl.multiple_of(start, 128)


def scores_space(q, k, v, u, shares, grads):
    def step(head, _):
        start = window(head)
        at = pl.ds(start, WIN)
        mask = head_mask(head, start, WIN)
        scores = dot_lanes(k[:, at] * mask, q[:, at])
        share_grad = dot_lanes(v[:, at] * mask, u[:, at])
        shares[head], grads[head] = softmax_and_grad(scores, share_grad)
        return 0

    lax.fori_loop(0, HEADS, step, 0, unroll=4)


def score_time(head, q, k, v, u, shares, grads):
    tokens = q.shape[0]
    half, frames = tokens // 2, tokens // CELL
    low = lax.broadcasted_iota(jnp.int32, (1, half), 1) < frames
    cell_of_lane = lax.broadcasted_iota(jnp.int32, (1, tokens), 1) // frames
    start = window(head)
    at = pl.ds(start, WIN)
    mask = head_mask(head, start, WIN)

    def compact(a, b):
        parts = []
        for i in range(2):
            rows = slice(i * half, (i + 1) * half)
            block = dot_lanes(a[rows, :], b[rows, :])
            parts.append(jnp.where(low, block[:frames, :], block[frames:, :]))
        return jnp.concatenate(parts, axis=1)

    def expand(block):
        zero = jnp.zeros_like(block)
        return jnp.concatenate([jnp.where(cell_of_lane == c, block, zero) for c in range(CELL)], axis=0)

    scores = compact(k[:, at] * mask, q[:, at])
    share_grad = compact(v[:, at] * mask, u[:, at])
    share, grad = softmax_and_grad(scores, share_grad)
    shares[head] = expand(share)
    grads[head] = expand(grad)


def gradients(first, heads, start, width, q, k, v, u, shares, grads, wanted=range(4)):
    at = pl.ds(start, width)
    totals = [None] * 4
    for i in range(heads):
        head = first + i
        mask = head_mask(head, start, width)
        for j in wanted:
            matrix = grads if j in (1, 2) else shares
            other = (v, k, q, u)[j]
            term = (dot_rows if j < 2 else dot)(matrix[head], other[:, at] * mask)
            totals[j] = term if totals[j] is None else totals[j] + term
    factor = 1.0 / math.sqrt(HEAD_DIM)
    return [totals[j] * factor if j in (1, 2) else totals[j] for j in wanted]


def to_slabs(source, target, count):
    def step(i, _):
        wide = source[pl.ds(pl.multiple_of(i * 16, 16), 16), :].astype(F32)
        for j in range(16 // CELL):
            target[i * (16 // CELL) + j] = wide[j * CELL : (j + 1) * CELL, :].astype(BF16)
        return 0

    lax.fori_loop(0, count * CELL // 16, step, 0, unroll=2)


def slabs_to_cells(source, wide):
    frames = source.shape[0]

    def step(f, _):
        slab = source[f].astype(F32)
        for t in range(D // 128):
            wide[t, pl.ds(f, CELL, stride=frames), :] = slab[:, t * 128 : (t + 1) * 128]
        return 0

    lax.fori_loop(0, frames, step, 0, unroll=8)


def kernel(
    n,
    tokens_total,
    qs_h,
    ks_h,
    vs_h,
    qt_h,
    kt_h,
    vt_h,
    cot_h,
    ws_h,
    wt_h,
    turn_h,
    first_x_h,
    first_y_h,
    second_h,
    gate_s,
    gate_t,
    dqs_o,
    dks_o,
    dvs_o,
    dqt_o,
    dkt_o,
    dvt_o,
    gws_o,
    gwt_o,
    qs,
    ks,
    vs,
    qraw,
    kraw,
    vraw,
    cot,
    ws,
    wt,
    turn,
    first_x,
    first_y,
    second,
    wide,
    parts,
    qt,
    kt,
    vt,
    cot_slabs,
    cot_got,
    gated,
    attended,
    up,
    shares,
    grads,
    spatial,
    temporal,
    sent_0,
    got_0,
    sent,
    got,
    far_a,
    far_g,
    product,
    turned,
    got_1x,
    got_1y,
    send_2x,
    send_2y,
    got_2x,
    got_2y,
    send_z,
    got_z,
    load_sem,
    store_sem,
    own_sem,
    cot_send,
    cot_recv,
    t_send,
    t_recv,
    w_send,
    w_recv,
    z_send,
    z_recv,
    pair_send,
    pair_recv,
):
    dp = lax.axis_index("dp")
    seq = lax.axis_index("seq")
    devices = n * n * n
    group, y = seq // n, seq % n
    x, z = group // n, group % n
    side, core = dp // 2, dp % 2
    sibling = dp + 1 - 2 * core
    tokens = devices * CELL
    split, half = got_1x.shape[2], product.shape[2]
    half_step = D - half

    loads = [
        pltpu.make_async_copy(source, target, load_sem.at[i])
        for i, (source, target) in enumerate(
            (
                (cot_h, cot),
                (ws_h, ws),
                (qs_h, qs),
                (ks_h, ks),
                (vs_h, vs),
                (qt_h, qraw),
                (kt_h, kraw),
                (vt_h, vraw),
                (wt_h, wt),
                (turn_h, turn),
                (first_x_h, first_x),
                (first_y_h, first_y),
                (second_h, second),
            )
        )
    ]
    for load in loads:
        load.start()

    def seq_peer(s):
        return (dp, s)

    def y_peer(yy):
        return (dp, group * n + yy)

    def x_peer(xx):
        return (dp, (xx * n + z) * n + y)

    def column_peer(q):
        return (q // n, (x * n + q % n) * n + y)

    barrier = pltpu.get_barrier_semaphore()

    def greet(device):
        pl.semaphore_signal(barrier, inc=1, device_id=device, device_id_type=MESH)

    def greet_seq(i, _):
        greet(seq_peer((seq + i) % devices))
        return 0

    lax.fori_loop(1, devices, greet_seq, 0)
    for i in range(1, 4):
        for zz in range(n):
            greet(column_peer((dp + i) % 4 * n + zz))
    loads[0].wait()
    to_slabs(cot, cot_slabs, devices)
    pl.semaphore_wait(barrier, devices - 1 + 3 * n)

    def remote(source, target, send, recv, device):
        return pltpu.make_async_remote_copy(
            src_ref=source,
            dst_ref=target,
            send_sem=send,
            recv_sem=recv,
            device_id=device,
            device_id_type=MESH,
        )

    def local(source, target, sem):
        return pltpu.make_async_copy(source, target, sem)

    def send_cot(i, _):
        peer = (seq + i) % devices
        remote(cot_slabs.at[peer], cot_got.at[seq], cot_send.at[0], cot_recv.at[0], seq_peer(peer)).start()
        return 0

    lax.fori_loop(1, devices, send_cot, 0)
    cot_own = local(cot_slabs.at[seq], cot_got.at[seq], own_sem.at[0])
    cot_own.start()

    gated[0] = (gate_s[...] * cot[...].astype(F32)).astype(BF16)

    def pair_gated(kind):
        k = 2 * kind
        lanes = pl.ds(pl.multiple_of((1 - core) * half_step, 128), half)
        return remote(
            gated.at[kind, :, lanes], far_g.at[kind], pair_send.at[k], pair_recv.at[k], (sibling, seq)
        )

    pair_gated(0).start()
    loads[1].wait()
    for start, width in lane_chunks(D, 384):
        project(gated.at[0], ws, up.at[0], start, width)
    for load in loads[2:5]:
        load.wait()
    space = (qs, ks, vs, up.at[0], shares.at[0], grads.at[0])
    scores_space(*space)
    whole = D // WIN
    tail = whole * WIN

    def space_attended(first, heads, start, width):
        (total,) = gradients(first, heads, start, width, *space, (0,))
        attended[0, :, pl.ds(start, width)] = total.astype(BF16)

    def space_window(first, heads, start, width):
        total = gradients(first, heads, start, width, *space, (1, 2, 3))
        for i in range(3):
            spatial[i, :, pl.ds(start, width)] = total[i].astype(BF16)

    def space_windows(window_of):
        def step(i, _):
            start = pl.multiple_of(i * WIN, 128)
            window_of(start // HEAD_DIM, CHUNK_HEADS, start, WIN)
            return 0

        lax.fori_loop(0, whole, step, 0)
        window_of(tail // HEAD_DIM, HEADS - tail // HEAD_DIM, tail, D - tail)

    space_windows(space_attended)

    def pair_attended(kind, i, at):
        k = 2 * kind + i
        return remote(
            attended.at[kind, :, at], far_a.at[kind, :, at], pair_send.at[k], pair_recv.at[k], (sibling, seq)
        )

    pair_attended(0, 1, slice(0, D)).start()

    for raw, target, load in ((qraw, qt, loads[5]), (kraw, kt, loads[6]), (vraw, vt, loads[7])):
        load.wait()
        slabs_to_cells(raw, wide)
        for t in range(D // 128):
            target[:, t * 128 : (t + 1) * 128] = wide[t].astype(BF16)

    def rows(ref, at, count):
        return ref.at[pl.ds(pl.multiple_of(at * count, 16 if count % 16 == 0 else 8), count)]

    def exchange(me, device, source, target, slot, size=n):
        copies = []
        for i in range(1, size):
            peer = (me + i) % size
            k = slot * n + i
            copies.append(remote(source(peer), target(me), w_send.at[k], w_recv.at[k], device(peer)))
        own = local(source(me), target(me), own_sem.at[1 + slot])
        return own, copies

    count_1, count_2 = D // n, send_2x.shape[1] // n
    lanes_1 = slice(0, split)

    def all_steps(kind):
        k = 4 * kind
        return (
            exchange(
                x,
                x_peer,
                lambda p: rows(product.at[kind], p, count_1).at[:, lanes_1],
                lambda p: rows(got_1x.at[kind], p, count_1),
                k,
            ),
            exchange(
                y,
                y_peer,
                lambda p: rows(turned.at[kind], p, count_1),
                lambda p: rows(got_1y.at[kind], p, count_1),
                k + 1,
            ),
            exchange(
                y,
                y_peer,
                lambda p: rows(send_2x.at[kind], p, count_2),
                lambda p: rows(got_2x.at[kind], p, count_2),
                k + 2,
            ),
            exchange(
                x,
                x_peer,
                lambda p: rows(send_2y.at[kind], p, count_2),
                lambda p: rows(got_2y.at[kind], p, count_2),
                k + 3,
            ),
        )

    steps = (all_steps(0), all_steps(1))

    owners = 2 * n
    to_self = core == side

    def owner_part(kind, e):
        return send_z.at[kind, e % n, :, :, pl.ds(pl.multiple_of(e // n * 256, 128), 384)]

    def owner_copy(kind, e):
        place = side * n + z
        return remote(
            owner_part(kind, e),
            got_z.at[kind, place],
            z_send.at[kind * owners + e],
            z_recv.at[kind * owners + place],
            column_peer((2 * core + e // n) * n + e % n),
        )

    def owner_own(kind):
        return local(owner_part(kind, core * n + z), got_z.at[kind, side * n + z], own_sem.at[9 + kind])

    def owner_each(first, use_own, use):
        @pl.when(to_self)
        def _():
            use_own()

        @pl.when(jnp.logical_not(to_self))
        def _():
            use(first)

        for i in range(1, owners):
            use((first + i) % owners)

    def begin_z(kind):
        owner_each(core * n + z, lambda: owner_own(kind).start(), lambda e: owner_copy(kind, e).start())

    def sent_z(kind):
        owner_each(core * n + z, lambda: None, lambda e: owner_copy(kind, e).wait_send())

    def arrived_z(kind):
        def wait(s):
            place = got_z.at[kind, s]
            local(place, place, z_recv.at[kind * owners + s]).wait()

        owner_each(side * n + z, lambda: owner_own(kind).wait(), wait)

    def begin(step):
        own, copies = step
        for copy in copies:
            copy.start()
        own.start()

    def arrived(step):
        own, copies = step
        own.wait()
        for copy in copies:
            copy.wait_recv()

    scale = 1.0 / math.sqrt(tokens_total)

    def product_rows(kind, first, blocks):
        def step(i, _):
            at = pl.ds(pl.multiple_of((first + i) * 128, 128), 128)
            for start, width in lane_chunks(half, 384):
                to = slice(start, start + width)
                near = gated[kind, :, pl.ds(pl.multiple_of(core * half_step + start, 128), width)]
                total = dot_rows(attended[kind, :, at], near) + dot_rows(far_a[kind, :, at], far_g[kind, :, to])
                product[kind, at, to] = (total * scale).astype(BF16)
            return 0

        lax.fori_loop(0, blocks, step, 0, unroll=math.gcd(blocks, 3) if blocks > 2 else blocks)

    def turn_product(kind):
        def turn_rows(i, _):
            at = pl.ds(pl.multiple_of(i * 128, 128), 128)
            turned[kind, at, :] = dot(turn[at, :], product[kind, :, split:]).astype(BF16)
            return 0

        lax.fori_loop(0, D // 128, turn_rows, 0, unroll=3)
        begin(steps[kind][1])

    def weight_second(kind):
        for at, matrix, source, target in ((0, first_x, got_1x, send_2x), (1, first_y, got_1y, send_2y)):
            arrived(steps[kind][at])
            target[kind] = dot(matrix[...], source[kind]).astype(BF16)
            begin(steps[kind][2 + at])

    def weight_third(kind):
        pad, count = second.shape[0] // n, send_z.shape[2]
        for at, source, base in ((2, got_2x, 0), (3, got_2y, split)):
            arrived(steps[kind][at])
            total = dot(second[...], source[kind]).astype(BF16)
            for i in range(n):
                for j in range(count):
                    row = i * pad + 2 * j
                    send_z[kind, i, j, :, base : base + total.shape[1]] = total[row : row + 2, :]
        begin_z(kind)

    def weight_last(kind, out):
        arrived_z(kind)
        total = functools.reduce(lambda a, b: a + b, (got_z[kind, s].astype(F32) for s in range(owners)))
        total = jnp.concatenate([total[j] for j in range(total.shape[0])], axis=0)
        width = out.shape[1]
        for i in range(4):

            @pl.when(dp == i)
            def _():
                base = i * width - i // 2 * half_step - i % 2 * 256
                out[...] = total[:, base : base + width]

    pair_gated(0).wait_recv()
    pair_attended(0, 1, slice(0, D)).wait_recv()
    product_rows(0, 0, D // 128)
    begin(steps[0][0])
    for load in loads[9:]:
        load.wait()
    turn_product(0)

    cot_own.wait()
    rest = pl.ds(0, devices - 1)
    local(cot_got.at[rest], cot_got.at[rest], cot_recv.at[0]).wait()
    slabs_to_cells(cot_got, wide)
    for t in range(D // 128):
        at = slice(t * 128, (t + 1) * 128)
        gated[1, :, at] = (gate_t[:, at] * wide[t]).astype(BF16)

    pair_gated(1).start()
    loads[8].wait()

    time = (qt, kt, vt, up.at[1], shares.at[1], grads.at[1])

    def time_attended(first, heads, start, width):
        at = pl.ds(start, width)
        (total,) = gradients(first, heads, start, width, *time, (0,))
        attended[1, :, at] = total.astype(BF16)

    def pieces(i, width):
        return (sent_0, got_0) if width == FIRST else (sent.at[i - 1], got.at[i - 1])

    def time_window(i, first, heads, start, width):
        total = gradients(first, heads, start, width, *time, (1, 2, 3))
        tiles = width // 128
        out, come = pieces(i, width)
        for t in range(3):
            for j in range(tiles):
                parts[t * tiles + j] = total[t][:, j * 128 : (j + 1) * 128]

        def narrow(f, _):
            for t in range(3):
                for j in range(tiles):
                    slab = parts[t * tiles + j, pl.ds(f, CELL, stride=devices), :]
                    out[f, t, :, j * 128 : (j + 1) * 128] = slab.astype(BF16)
            return 0

        lax.fori_loop(0, devices, narrow, 0, unroll=8)

        def send(k, _):
            peer = (seq + k) % devices
            remote(out.at[peer], come.at[seq], t_send.at[i], t_recv.at[i], seq_peer(peer)).start()
            return 0

        lax.fori_loop(1, devices, send, 0)
        local(out.at[seq], come.at[seq], own_sem.at[11 + i]).start()

    def time_scores(first, count):
        def step(i, _):
            score_time(first + i, *time)
            return 0

        lax.fori_loop(0, count, step, 0, unroll=count if count < 5 else count // 2)

    def place_of(i):
        start = pl.multiple_of((i - 1) * WIN + FIRST, 128)
        return jnp.minimum(start // HEAD_DIM, HEADS - CHUNK_HEADS), CHUNK_HEADS, start, WIN

    opening = (0, -(-FIRST // HEAD_DIM), 0, FIRST)
    early = (slice(0, FIRST), slice(FIRST, D))

    project(gated.at[1], wt, up.at[1], 0, 256)
    time_scores(0, opening[1])
    time_window(0, *opening)

    project(gated.at[1], wt, up.at[1], 256, 512)
    time_scores(opening[1], CHUNK_HEADS + 1 - opening[1])
    time_window(1, *place_of(1))

    project(gated.at[1], wt, up.at[1], 768, 384)
    time_scores(CHUNK_HEADS + 1, HEADS - CHUNK_HEADS - 1)
    time_attended(*opening)
    pair_attended(1, 1, early[0]).start()

    def attended_step(i, _):
        time_attended(*place_of(i))
        return 0

    lax.fori_loop(1, whole + 1, attended_step, 0)
    pair_attended(1, 2, early[1]).start()
    time_window(2, *place_of(2))
    pair_gated(1).wait_recv()
    for i, at in enumerate(early):
        pair_attended(1, 1 + i, at).wait_recv()
    product_rows(1, 0, D // 128)
    begin(steps[1][0])
    turn_product(1)
    weight_second(0)

    def window_step(i, _):
        time_window(i, *place_of(i))
        return 0

    lax.fori_loop(3, whole + 1, window_step, 0)
    weight_third(0)
    weight_second(1)
    space_windows(space_window)
    space_stores = [local(spatial.at[i], out, store_sem.at[i]) for i, out in enumerate((dqs_o, dks_o, dvs_o))]
    for store in space_stores:
        store.start()
    weight_third(1)
    weight_last(0, gws_o)

    outs = (dqt_o, dkt_o, dvt_o)
    stores = [(temporal.at[i], out) for i, out in enumerate(outs)]
    final = []
    for i in range(whole + 1):
        start, width = (0, FIRST) if i == 0 else ((i - 1) * WIN + FIRST, WIN)
        at = slice(start, start + width)
        out, come = pieces(i, width)
        local(out.at[seq], come.at[seq], own_sem.at[11 + i]).wait()
        local(come.at[rest], come.at[rest], t_recv.at[i]).wait()

        def join(k, _):
            for t in range(3):
                slabs = [come[k * (16 // CELL) + j, t].astype(F32) for j in range(16 // CELL)]
                to = pl.ds(pl.multiple_of(k * 16, 16), 16)
                temporal[t, to, at] = jnp.concatenate(slabs, axis=0).astype(BF16)
            return 0

        lax.fori_loop(0, tokens // 16, join, 0, unroll=2)
        for t, (source, target) in enumerate(stores):
            final.append(local(source.at[:, at], target.at[:, at], store_sem.at[3 + 3 * i + t]))
            final[-1].start()

    weight_last(1, gwt_o)
    for store in space_stores + final:
        store.wait()
    local(cot_slabs.at[rest], cot_slabs.at[rest], cot_send.at[0]).wait()
    for i in range(whole + 1):
        out, _ = pieces(i, FIRST if i == 0 else WIN)
        local(out.at[rest], out.at[rest], t_send.at[i]).wait()
    for kind in range(2):
        for _, copies in steps[kind]:
            for copy in copies:
                copy.wait_send()
        sent_z(kind)
        pair_gated(kind).wait_send()
    pair_attended(0, 1, slice(0, D)).wait_send()
    for i, at in enumerate(early):
        pair_attended(1, 1 + i, at).wait_send()


def hand_over(*refs):
    sources, targets, buffers, (in_sem, out_sem) = refs[:6], refs[6:12], refs[12:18], refs[18:]
    steps = [
        (pltpu.make_async_copy(s, b, in_sem.at[i]), pltpu.make_async_copy(b, t, out_sem.at[i]))
        for i, (s, b, t) in enumerate(zip(sources, buffers, targets))
    ]
    for come, _ in steps:
        come.start()
    for come, go in steps:
        come.wait()
        go.start()
    for _, go in steps:
        go.wait()


def per_device(n, maps, qs, ks, vs, qt, kt, vt, cot, gate_s, gate_t, ws, wt):
    tokens = cot.shape[2]
    frames = qt.shape[1]
    devices = n * n * n
    rows_z = D // devices
    pad_y = padded(D // n // n)
    split, half = 384, D // 2 + 64
    shape = cot.shape
    flat = lambda a: a.reshape(tokens, D)
    cells = lambda a: a.reshape(frames, CELL, D)
    any_space = pl.BlockSpec(memory_space=pl.ANY)
    vmem = pl.BlockSpec(memory_space=pltpu.VMEM)
    token = pltpu.VMEM((tokens, D), BF16)
    tokens_of = lambda k: pltpu.VMEM((k, tokens, D), BF16)
    raw = pltpu.VMEM((frames, CELL, D), BF16)
    weight = pltpu.VMEM((D, D), BF16)
    dma = lambda k: pltpu.SemaphoreType.DMA((k,))
    array = lambda *dims: pltpu.VMEM(dims, BF16)
    total = 4 * devices * tokens
    windows = 1 + (D - FIRST) // WIN
    result = pl.pallas_call(
        functools.partial(kernel, n, total),
        out_shape=[jax.ShapeDtypeStruct((tokens, D), BF16)] * 6
        + [jax.ShapeDtypeStruct((rows_z, D // 4), F32)] * 2,
        in_specs=[any_space] * 13 + [vmem] * 2,
        out_specs=[any_space] * 6 + [vmem] * 2,
        scratch_shapes=[token] * 3
        + [raw] * 3
        + [token]
        + [weight] * 2
        + [pltpu.VMEM(m.shape, BF16) for m in maps]
        + [pltpu.VMEM((D // 128, tokens, 128), F32), pltpu.VMEM((3 * WIN // 128, tokens, 128), F32)]
        + [token] * 3
        + [raw] * 2
        + [tokens_of(2)] * 2
        + [tokens_of(2)]
        + [array(2, HEADS, tokens, tokens)] * 2
        + [tokens_of(3)] * 2
        + [array(devices, 3, CELL, FIRST)] * 2
        + [array(windows - 1, devices, 3, CELL, WIN)] * 2
        + [tokens_of(2), array(2, tokens, half)]
        + [array(2, D, half), array(2, D, half - split), array(2, D, split), array(2, D, half - split)]
        + [array(2, n * pad_y, split), array(2, n * pad_y, half - split)] * 2
        + [array(2, n, rows_z // 2, 2, half), array(2, 2 * n, rows_z // 2, 2, 384)]
        + [dma(13), dma(3 + 3 * windows), dma(11 + windows)]
        + [dma(1)] * 2
        + [dma(windows)] * 2
        + [dma(8 * n)] * 2
        + [dma(4 * n)] * 2
        + [dma(5)] * 2,
        compiler_params=pltpu.CompilerParams(
            collective_id=0, has_side_effects=True, vmem_limit_bytes=60 * 1024 * 1024
        ),
    )(flat(qs), flat(ks), flat(vs), cells(qt), cells(kt), cells(vt), flat(cot), ws, wt, *maps, gate_s, gate_t)
    tensors = pl.pallas_call(
        hand_over,
        out_shape=[jax.ShapeDtypeStruct((tokens, D), BF16)] * 6,
        in_specs=[any_space] * 6,
        out_specs=[any_space] * 6,
        scratch_shapes=[token] * 6 + [dma(6)] * 2,
    )(*result[:6])
    return tuple(a.reshape(shape) for a in tensors) + tuple(result[6:])


def solution(mesh):
    n = round(mesh.shape["seq"] ** (1 / 3))
    maps = row_maps(n)
    frames = P("dp", "seq", None, None)
    cells = P("dp", None, "seq", None)

    def run(*args):
        return per_device(n, [jnp.asarray(m) for m in maps], *args)

    return jax.shard_map(
        run,
        mesh=mesh,
        in_specs=(frames,) * 3 + (cells,) * 3 + (frames, P("dp", None), P("dp", None), P(), P()),
        out_specs=(frames,) * 6 + (P("seq", "dp"),) * 2,
        check_vma=False,
    )
```
